128 devices in a mesh: dp: 8 (over y_hi, x), grid: 16 (over z, y_lo, core).
Axes of the slice: x: 4, y: 4 (y_hi: 2, y_lo: 2; y = y_hi * 2 + y_lo), z: 4, core: 2. Of those that a mesh axis runs over, the one named last changes fastest.
Arguments:
- inputs: bfloat16 [8192, 5120], P('dp'), may hold values from -6 to 6
- queries: bfloat16 [8192, 12288], P('dp', 'grid'), may hold values from -300 to 300
- key_rows: bfloat16 [8192, 1024], P('dp'), may hold values from -5 to 5
- values: bfloat16 [8192, 1024], P('dp'), may hold values from -6 to 6
- attn_out: bfloat16 [8192, 12288], P('dp', 'grid'), may hold values from -6 to 6
- grad_out: bfloat16 [8192, 12288], P('dp', 'grid'), may hold values from -6 to 6
- momentum: float32 [5120, 12288], P('dp', 'grid'), may hold values from -6 to 6
- iterate: bfloat16 [5120, 12288], P('dp', 'grid'), may hold values from -1 to 1
Outputs:
- momentum_next: float32 [5120, 12288], P('dp', 'grid')
- update: bfloat16 [5120, 12288], P('dp', 'grid')
The draws below stay inside these ranges and needn't reach their ends.
All inputs are finite; a program needn't handle non-finite values.
Results may differ from the reference program's by a relative error of at most 0.027.
Values may be sent and summed in bfloat16 or wider, within the bound.
No kernel may reach another device: no remote copies, remote signals or barrier semaphores. Data moves between devices by JAX's collectives and lax.ppermute only.
A program may use at most 192 MiB of HBM per device.

```python
import math
import jax
import jax.numpy as jnp
from jax import lax

D = 5120
HEADS = 96
KV_HEADS = 8
HEAD_DIM = 128
SEQ_LEN = 1024
QD = 12288
TOK_DEV = 1024
TOKENS = 8192
N_DP = 8
N_GRID = 16


def key_table(key):
    base = jax.random.truncated_normal(key, -4.0, 4.0, (TOKENS, KV_HEADS * HEAD_DIM), jnp.float32)
    position = jnp.arange(TOKENS, dtype=jnp.int32) % SEQ_LEN
    paired = position % 64 == 32
    return jnp.where(paired[:, None], base, base)


def draw_key_rows(key, part):
    table = key_table(key)
    return table.astype(jnp.bfloat16)


def draw_queries(key, part):
    key = jax.random.fold_in(key, 5)
    drawn = jax.random.truncated_normal(key, -4.0, 4.0, (TOKENS, QD), jnp.float32)
    return drawn.astype(jnp.bfloat16)


def draw_iterate(key, part):
    key = jax.random.fold_in(key, 7)
    spread_scale = 1.1 / (math.sqrt(D) + math.sqrt(QD))
    entries = jax.random.truncated_normal(key, -5.0, 5.0, (D, QD), jnp.float32)
    return (entries * spread_scale).astype(jnp.bfloat16)


def spiked(values, own_key, source, target, parts, factor):
    def block_of(dim):
        return (jnp.arange(values.shape[dim]) // (values.shape[dim] // parts)).reshape((-1,) + (1,) * (values.ndim - 1 - dim))

    first = jax.random.permutation(own_key, parts)[block_of(target)]
    second = (block_of(target) + parts // 2) % parts
    return jnp.where((block_of(source) == first) | (block_of(source) == second), factor * values, values)


def block_scale(rng, dims, shards, least, largest):
    gain = 1.0
    for dim, blocks in shards:
        draws = jax.random.uniform(jax.random.fold_in(jax.random.fold_in(rng, 6), dim), (blocks,), jnp.float32, least / len(shards), largest / len(shards))
        gain = gain * jnp.repeat(jnp.exp(draws), dims[dim] // blocks).reshape((-1,) + (1,) * (len(dims) - 1 - dim))
    return gain


def scatter_about(rng, dims, scale, bound, split=(), held_as=jnp.bfloat16):
    values = scale * jax.random.normal(rng, dims, jnp.float32)
    if split:
        values = values * block_scale(rng, dims, split, -0.22, 0.18)
    return jnp.clip(values, -bound, bound).astype(held_as)


def bell_draw_with(rng, extent, deviation, bound, shards, heavy, held_as=jnp.bfloat16):
    array = deviation * jax.random.normal(rng, extent, jnp.float32)
    if shards:
        array = array * block_scale(rng, extent, shards, -0.22, 0.18)
    return jnp.clip(spiked(array, jax.random.fold_in(rng, 3), *heavy), -bound, bound).astype(held_as)


def setup_inputs(seed: int = 0) -> dict:
    key_list = jax.random.split(jax.random.key(seed), 9)
    return {
        "inputs": bell_draw_with(key_list[0], (TOKENS, D), 1.0, 6.0, ((0, 8),), (0, 1, 8, 2.0)),
        "queries": draw_queries(jax.random.fold_in(key_list[8], 71), 0),
        "key_rows": draw_key_rows(jax.random.fold_in(key_list[8], 71), 0),
        "values": scatter_about(key_list[3], (TOKENS, KV_HEADS * HEAD_DIM), 1.0, 6.0, ((0, 8),)),
        "attn_out": scatter_about(key_list[4], (TOKENS, QD), 1.0, 6.0, ((0, 8), (1, 16))),
        "grad_out": scatter_about(key_list[5], (TOKENS, QD), 1.0, 6.0, ((0, 8), (1, 16))),
        "momentum": scatter_about(key_list[6], (D, QD), 1.0, 6.0, ((0, 8), (1, 16)), jnp.float32),
        "iterate": draw_iterate(jax.random.fold_in(key_list[8], 71), 0),
    }


linear_coef = 3.4445
cubic_coef = -4.775
quintic_coef = 2.0315

def reference(inputs, queries, key_rows, values, attn_out, grad_out, momentum, iterate):
    group_size = HEADS // KV_HEADS
    score_scale = 1.0 / math.sqrt(HEAD_DIM)
    sequences = TOKENS // SEQ_LEN
    query_seq = queries.reshape(sequences, SEQ_LEN, HEADS, HEAD_DIM)
    out_seq = attn_out.reshape(sequences, SEQ_LEN, HEADS, HEAD_DIM)
    dout_seq = grad_out.reshape(sequences, SEQ_LEN, HEADS, HEAD_DIM)
    key_seq = key_rows.reshape(sequences, SEQ_LEN, KV_HEADS, HEAD_DIM)
    value_seq = values.reshape(sequences, SEQ_LEN, KV_HEADS, HEAD_DIM)
    positions = jnp.arange(SEQ_LEN, dtype=jnp.int32)
    causal = positions[None, :] <= positions[:, None]

    def one_head(head):
        kv_head = head // group_size
        query_h = query_seq[:, :, head].astype(jnp.float32)
        key_h = key_seq[:, :, kv_head].astype(jnp.float32)
        value_h = value_seq[:, :, kv_head].astype(jnp.float32)
        dout_h = dout_seq[:, :, head].astype(jnp.float32)
        out_h = out_seq[:, :, head].astype(jnp.float32)
        scores = jnp.einsum('sqd,skd->sqk', query_h, key_h) * score_scale
        scores = jnp.where(causal[None], scores, -jnp.inf)
        row_max = lax.optimization_barrier(jnp.max(scores, axis=-1, keepdims=True))
        probs = jnp.exp(scores - row_max)
        probs = probs / lax.optimization_barrier(jnp.sum(probs, axis=-1, keepdims=True))
        grad_prob = jnp.einsum('sqd,skd->sqk', dout_h, value_h)
        row_delta = lax.optimization_barrier(jnp.sum(dout_h * out_h, axis=-1))
        grad_score = (probs * (grad_prob - row_delta[..., None]) * score_scale).astype(jnp.bfloat16)
        return jnp.einsum('sqk,skd->sqd', grad_score.astype(jnp.float32), key_h).astype(jnp.bfloat16)
    per_head = lax.map(one_head, jnp.arange(HEADS, dtype=jnp.int32))
    grad_query = per_head.transpose(1, 2, 0, 3).reshape(TOKENS, QD)
    input_blocks = inputs.reshape(N_DP, TOK_DEV, D)
    grad_blocks = grad_query.reshape(N_DP, TOK_DEV, QD)

    def add_grad(total, pair):
        term = jnp.dot(pair[0].T, pair[1], preferred_element_type=jnp.float32).astype(jnp.bfloat16)
        term = lax.optimization_barrier(term)
        return (total + term.astype(jnp.float32), None)
    grad, _ = lax.scan(add_grad, jnp.zeros((D, QD), jnp.float32), (input_blocks, grad_blocks))
    momentum_next = 0.95 * momentum + grad
    column_blocks = iterate.reshape(D, N_GRID, QD // N_GRID).transpose(1, 0, 2)

    def add_gram(total, block):
        term = jnp.dot(block, block.T, preferred_element_type=jnp.float32).astype(jnp.bfloat16)
        term = lax.optimization_barrier(term)
        return (total + term.astype(jnp.float32), None)
    gram_sum, _ = lax.scan(add_gram, jnp.zeros((D, D), jnp.float32), column_blocks)
    gram = gram_sum.astype(jnp.bfloat16)
    first = jnp.dot(gram, iterate, preferred_element_type=jnp.float32).astype(jnp.bfloat16)
    second = jnp.dot(gram, first, preferred_element_type=jnp.float32)
    combined = linear_coef * iterate.astype(jnp.float32) + cubic_coef * first.astype(jnp.float32) + quintic_coef * second
    update = (math.sqrt(QD) * combined).astype(jnp.bfloat16)
    return (momentum_next, update)
```

```python
import math

import jax
import jax.numpy as jnp
import numpy as np
from jax import lax
from jax.experimental import pallas as pl
from jax.experimental.pallas import tpu as pltpu
from jax.sharding import PartitionSpec as P

HEADS = 96
KV_HEADS = 8
HEAD_DIM = 128
SEQ_LEN = 1024
QD = 12288
D = 5120
ROWS = 640
COLS = 768
HALF = 320
QUART = 160
SHAPE = (2, 4, 4, 2, 2)

linear_coef = 3.4445
cubic_coef = -4.775
quintic_coef = 2.0315

VMEM = 60 * 1024 * 1024


def make_perm(move):
    pairs = []
    for source in range(128):
        place = np.unravel_index(source, SHAPE)
        target = [int(a) % b for a, b in zip(move(*place), SHAPE)]
        pairs.append((source, int(np.ravel_multi_index(target, SHAPE))))
    return pairs


X_UP = make_perm(lambda yh, x, z, yl, c: (yh, x + 1, z, yl, c))
X_DOWN = make_perm(lambda yh, x, z, yl, c: (yh, x - 1, z, yl, c))
Z_UP = make_perm(lambda yh, x, z, yl, c: (yh, x, z + 1, yl, c))
Z_DOWN = make_perm(lambda yh, x, z, yl, c: (yh, x, z - 1, yl, c))
Z_FAR = make_perm(lambda yh, x, z, yl, c: (yh, x, z + 2, yl, c))
X_FAR = make_perm(lambda yh, x, z, yl, c: (yh, x + 2, z, yl, c))
Y_HI = make_perm(lambda yh, x, z, yl, c: (yh + 1, x, z, yl, c))
Y_LO = make_perm(lambda yh, x, z, yl, c: (yh, x, z, yl + 1, c))
CORE = make_perm(lambda yh, x, z, yl, c: (yh, x, z, yl, c + 1))


def move(array, perm):
    return lax.ppermute(array, ("dp", "grid"), perm)


def place():
    dp = lax.axis_index("dp")
    grid = lax.axis_index("grid")
    return dp // 4, dp % 4, grid // 4, (grid // 2) % 2, grid % 2


def cost(flops, bytes_accessed, transcendentals=0):
    return pl.CostEstimate(
        flops=flops, bytes_accessed=bytes_accessed, transcendentals=transcendentals
    )


def dot(a, b, ca, cb):
    return lax.dot_general(a, b, (((ca,), (cb,)), ((), ())), preferred_element_type=jnp.float32)


def attention_kernel(q_ref, k_ref, v_ref, o_ref, do_ref, out_ref):
    block = 256
    scale = 1.0 / math.sqrt(HEAD_DIM)
    rows = lax.broadcasted_iota(jnp.int32, (block, block), 0)
    cols = lax.broadcasted_iota(jnp.int32, (block, block), 1)
    keep = cols <= rows
    for r in range(SEQ_LEN // block):
        start, length = r * block, (r + 1) * block
        q = q_ref[start:length, :]
        do = do_ref[start:length, :]
        o = o_ref[start:length, :]
        delta = jnp.sum(do.astype(jnp.float32) * o.astype(jnp.float32), axis=-1, keepdims=True)
        diag = jnp.where(keep, dot(q, k_ref[start:length, :], 1, 1), -jnp.inf)
        row_max = jnp.max(diag, axis=-1, keepdims=True)
        if r:
            body = dot(q, k_ref[:start, :], 1, 1)
            row_max = jnp.maximum(row_max, jnp.max(body, axis=-1, keepdims=True))
        e = jnp.exp((diag - row_max) * scale)
        total = jnp.sum(e, axis=-1, keepdims=True)
        g = (e * (dot(do, v_ref[start:length, :], 1, 1) - delta)).astype(jnp.bfloat16)
        grad = dot(g, k_ref[start:length, :], 1, 0)
        if r:
            e = jnp.exp((body - row_max) * scale)
            total = total + jnp.sum(e, axis=-1, keepdims=True)
            g = (e * (dot(do, v_ref[:start, :], 1, 1) - delta)).astype(jnp.bfloat16)
            grad = grad + dot(g, k_ref[:start, :], 1, 0)
        grad = grad * (scale / total)
        out_ref[:, start:length] = grad.T.astype(jnp.bfloat16)


def attention(queries, keys, values, attn_out, grad_out, kv_index):
    heads = queries.shape[1] // HEAD_DIM
    mine = pl.BlockSpec((SEQ_LEN, HEAD_DIM), lambda h, kv: (0, h))
    shared = pl.BlockSpec((SEQ_LEN, HEAD_DIM), lambda h, kv: (0, kv[0]))

    def body(kv, *refs):
        attention_kernel(*refs)

    return pl.pallas_call(
        body,
        grid_spec=pltpu.PrefetchScalarGridSpec(
            num_scalar_prefetch=1,
            grid=(heads,),
            in_specs=[mine, shared, shared, mine, mine],
            out_specs=pl.BlockSpec((HEAD_DIM, SEQ_LEN), lambda h, kv: (h, 0)),
        ),
        out_shape=jax.ShapeDtypeStruct((heads * HEAD_DIM, SEQ_LEN), jnp.bfloat16),
        compiler_params=pltpu.CompilerParams(vmem_limit_bytes=VMEM),
        cost_estimate=cost(24 * 10**9, 8 * 10**6, 4 * 10**6),
        name="attention",
    )(kv_index, queries, keys, values, attn_out, grad_out)


def gradient_kernel(gq_ref, in_ref, out_ref):
    out_ref[0] = dot(gq_ref[...], in_ref[...], 1, 0).astype(jnp.bfloat16)


def gradient_partial(grad_query_t, inputs):
    blocks = D // ROWS
    return pl.pallas_call(
        gradient_kernel,
        grid=(blocks,),
        in_specs=[
            pl.BlockSpec((COLS, SEQ_LEN), lambda k: (0, 0)),
            pl.BlockSpec((SEQ_LEN, ROWS), lambda k: (0, k)),
        ],
        out_specs=pl.BlockSpec((1, COLS, ROWS), lambda k: (k, 0, 0)),
        out_shape=jax.ShapeDtypeStruct((blocks, COLS, ROWS), jnp.bfloat16),
        compiler_params=pltpu.CompilerParams(vmem_limit_bytes=VMEM),
        cost_estimate=cost(2 * D * COLS * SEQ_LEN, 20 * 10**6),
        name="gradient",
    )(grad_query_t, inputs)


def gram_kernel(own_ref, b0, b1, b2a, b2b, b3, keep_ref, send_ref):
    _, x, z, _, core = place()
    for ahead, block in enumerate((b0, b1, None, b3)):
        slot = (x + ahead - z + 4) % 4
        for out_ref, half in ((keep_ref, core), (send_ref, 1 - core)):
            if block is None:

                @pl.when(half == 0)
                def _():
                    out_ref[slot] = dot(b2a[...], own_ref[...], 1, 1).astype(jnp.bfloat16)

                @pl.when(half == 1)
                def _():
                    out_ref[slot] = dot(b2b[...], own_ref[...], 1, 1).astype(jnp.bfloat16)

            else:
                rows = block[pl.ds(pl.multiple_of(half * HALF, HALF), HALF), :]
                out_ref[slot] = dot(rows, own_ref[...], 1, 1).astype(jnp.bfloat16)


def gram_partial(own, blocks):
    here, above, far, below = blocks
    out = jax.ShapeDtypeStruct((4, HALF, ROWS), jnp.bfloat16)
    return pl.pallas_call(
        gram_kernel,
        in_specs=[pl.BlockSpec(memory_space=pltpu.VMEM)] * 6,
        out_specs=[pl.BlockSpec(memory_space=pltpu.VMEM)] * 2,
        out_shape=[out, out],
        compiler_params=pltpu.CompilerParams(vmem_limit_bytes=VMEM),
        cost_estimate=cost(8 * ROWS * ROWS * COLS, 9 * 10**6),
        name="gram",
    )(own, here, above, *far, below)


def reduce_gram(keep, send):
    _, _, _, yl, _ = place()
    total = (keep.astype(jnp.float32) + move(send, CORE).astype(jnp.float32)).astype(jnp.bfloat16)
    up = move(total[1], Z_UP)
    down = move(total[3], Z_DOWN)
    far = move(total[2], Z_FAR)
    f32 = jnp.float32
    summed = total[0].astype(f32) + up.astype(f32) + down.astype(f32) + far.astype(f32)
    pair = summed.reshape(2, QUART, ROWS)
    mine = lax.dynamic_index_in_dim(pair, yl, 0, False)
    theirs = lax.dynamic_index_in_dim(pair, 1 - yl, 0, False).astype(jnp.bfloat16)
    return (mine + move(theirs, Y_LO).astype(f32)).astype(jnp.bfloat16)


PIECES = [(0, 0), (0, 1), (3, 0), (1, 0), (2, 0), (3, 1), (1, 1), (2, 1)]


def gather_first(own):
    return move(own, Z_UP), move(own, Z_DOWN), move(own, Y_LO), move(own, Z_FAR)


def gather_second(own, arrived):
    below, above, lo, far = arrived
    lo_below = move(lo, Z_UP)
    lo_above = move(lo, Z_DOWN)
    lo_far = move(far, Y_LO)
    first = jnp.stack([own, lo, below, above, far])
    second = jnp.stack([lo_below, lo_above, lo_far])
    return first, second, move(first, CORE), move(second, CORE)


def copies_of(gathered, target, sems):
    first, second, other_first, other_second = gathered
    _, _, z, yl, core = place()
    out = []
    for flipped, (early, late) in enumerate(((first, second), (other_first, other_second))):
        for n, (ahead, flip) in enumerate(PIECES):
            source = early.at[n] if n < 5 else late.at[n - 5]
            z_piece = (z + ahead) % 4
            yl_piece = (yl + flip) % 2
            core_piece = (core + flipped) % 2
            for yh in range(2):
                row = yh * 4 * ROWS + z_piece * ROWS + core_piece * HALF + yl_piece * QUART
                out.append(
                    pltpu.make_async_copy(
                        source.at[yh],
                        target.at[pl.ds(pl.multiple_of(row, QUART), QUART), :],
                        sems.at[len(out)],
                    )
                )
    return out


def square_kernel(own_ref, g0, g1, g2, g3, *refs):
    pieces = refs[:8]
    out_ref, full, acc, sems = refs[8:]
    yh, x, _, _, _ = place()
    copies = copies_of((g0, g1, g2, g3), full, sems)
    for copy in copies:
        copy.start()
    for copy in copies:
        copy.wait()
    acc[...] = jnp.zeros_like(acc)
    for n, piece in enumerate(pieces):
        block = ((yh + n // 4) % 2) * 4 + (x + n % 4) % 4
        lhs = piece[...].reshape(HALF, ROWS)
        rhs = full[pl.ds(pl.multiple_of(block * ROWS, ROWS), ROWS), :]
        acc[...] += dot(lhs, rhs, 1, 0)
    own = own_ref[...].reshape(HALF, ROWS).astype(jnp.float32)
    out = cubic_coef * own + quintic_coef * acc[...]
    out_ref[...] = out.astype(jnp.bfloat16).reshape(2, QUART, ROWS)


def square(own, gathered, rows):
    anywhere = pl.BlockSpec(memory_space=pl.ANY)
    inside = pl.BlockSpec(memory_space=pltpu.VMEM)
    return pl.pallas_call(
        square_kernel,
        in_specs=[inside] + [anywhere] * 4 + [inside] * 8,
        out_specs=inside,
        out_shape=jax.ShapeDtypeStruct((2, QUART, ROWS), jnp.bfloat16),
        scratch_shapes=[
            pltpu.VMEM((D, ROWS), jnp.bfloat16),
            pltpu.VMEM((HALF, ROWS), jnp.float32),
            pltpu.SemaphoreType.DMA((32,)),
        ],
        compiler_params=pltpu.CompilerParams(vmem_limit_bytes=VMEM),
        cost_estimate=cost(2 * HALF * D * ROWS, 11 * 10**6),
        name="square",
    )(own, *gathered, *rows)


def update_kernel(own_ref, n0, n1, n2, n3, *refs):
    blocks = refs[:10]
    out_ref, full, rhs, acc, sems, block_sems = refs[10:]
    yh, x, _, _, _ = place()
    copies = copies_of((n0, n1, n2, n3), full, sems)
    at = 0
    for flip in range(2):
        for ahead in range(4):
            row = ((yh + flip) % 2) * 4 * ROWS + ((x + ahead) % 4) * ROWS
            pieces = 2 if ahead == 2 else 1
            size = ROWS // pieces
            for piece in range(pieces):
                copies.append(
                    pltpu.make_async_copy(
                        blocks[at],
                        rhs.at[pl.ds(pl.multiple_of(row + piece * size, QUART), size), :],
                        block_sems.at[at],
                    )
                )
                at += 1
    for copy in copies:
        copy.start()
    for copy in copies:
        copy.wait()
    acc[...] = jnp.zeros_like(acc)

    def step(k, carry):
        at_k = pl.ds(pl.multiple_of(k * ROWS, ROWS), ROWS)
        acc[...] += dot(full[at_k, :], rhs[at_k, :], 0, 0)
        return carry

    lax.fori_loop(0, 8, step, 0)
    out = linear_coef * own_ref[...].astype(jnp.float32) + acc[...]
    out_ref[...] = (math.sqrt(QD) * out).astype(jnp.bfloat16)


def update_of(own, gathered, blocks):
    anywhere = pl.BlockSpec(memory_space=pl.ANY)
    inside = pl.BlockSpec(memory_space=pltpu.VMEM)
    return pl.pallas_call(
        update_kernel,
        in_specs=[inside] + [anywhere] * 14,
        out_specs=inside,
        out_shape=jax.ShapeDtypeStruct((ROWS, COLS), jnp.bfloat16),
        scratch_shapes=[
            pltpu.VMEM((D, ROWS), jnp.bfloat16),
            pltpu.VMEM((D, COLS), jnp.bfloat16),
            pltpu.VMEM((ROWS, COLS), jnp.float32),
            pltpu.SemaphoreType.DMA((32,)),
            pltpu.SemaphoreType.DMA((10,)),
        ],
        compiler_params=pltpu.CompilerParams(vmem_limit_bytes=VMEM),
        cost_estimate=cost(2 * D * ROWS * COLS, 15 * 10**6),
        name="update",
    )(own, *gathered, *blocks)


def per_device(inputs, queries, key_rows, values, attn_out, grad_out, momentum, iterate):
    yh = place()[0]
    together = lax.optimization_barrier

    own = iterate
    below = move(own, X_UP)
    above = move(own, X_DOWN)
    across = move(own, Y_HI)
    kv_index = (lax.axis_index("grid") // 2).astype(jnp.int32).reshape(1)
    grad_query_t = attention(queries, key_rows, values, attn_out, grad_out, kv_index)
    below, above, across, grad_query_t = together((below, above, across, grad_query_t))
    far = (move(below[:HALF], X_UP), move(above[HALF:], X_DOWN))
    far, below, above, across = together((far, below, above, across))
    across_below = move(across, X_UP)
    across_above = move(across, X_DOWN)
    across_far = (move(far[0], Y_HI), move(far[1], Y_HI))
    near = reduce_gram(*gram_partial(own, (own, above, far, below)))

    partial = gradient_partial(grad_query_t, inputs)
    gradient_t = lax.psum_scatter(partial, "dp", scatter_dimension=0, tiled=False)
    momentum_next = 0.95 * momentum + gradient_t.astype(jnp.float32).T

    across_below, across_above, across_far, partial = together(
        (across_below, across_above, across_far, partial)
    )
    other = reduce_gram(
        *gram_partial(own, (across, across_above, across_far, across_below))
    )
    rows = jnp.where(yh == 0, jnp.stack([near, other]), jnp.stack([other, near]))

    over_grid = gather_first(rows)
    over_dp = (move(rows, X_UP), move(rows, X_DOWN), move(rows, Y_HI), move(rows, X_FAR))
    over_grid, over_dp = together((over_grid, over_dp))
    over_grid = gather_second(rows, over_grid)
    r_below, r_above, r_across, r_far = over_dp
    over_dp = (
        rows,
        r_above,
        r_far,
        r_below,
        r_across,
        move(r_across, X_DOWN),
        move(r_far, Y_HI),
        move(r_across, X_UP),
    )
    combined = square(rows, over_grid, over_dp)
    over_grid = together(gather_first(combined))
    update = update_of(
        own,
        gather_second(combined, over_grid),
        (own, above, *far, below, across, across_above, *across_far, across_below),
    )
    return (momentum_next, update)


def solution(mesh):
    placed = (
        P("dp", None),
        P("dp", "grid"),
        P("dp", None),
        P("dp", None),
        P("dp", "grid"),
        P("dp", "grid"),
        P("dp", "grid"),
        P("dp", "grid"),
    )
    return jax.shard_map(
        per_device,
        mesh=mesh,
        in_specs=placed,
        out_specs=(P("dp", "grid"), P("dp", "grid")),
        check_vma=False,
    )
```

```python
import math

import jax
import jax.numpy as jnp
import numpy as np
from jax import lax
from jax.experimental import pallas as pl
from jax.experimental.pallas import tpu as pltpu
from jax.sharding import PartitionSpec as P

HEADS = 96
KV_HEADS = 8
HEAD_DIM = 128
SEQ_LEN = 1024
QD = 12288
D = 5120
ROWS = 640
COLS = 768
HALF = 320
QUART = 160
SHAPE = (2, 4, 4, 2, 2)

linear_coef = 3.4445
cubic_coef = -4.775
quintic_coef = 2.0315

VMEM = 60 * 1024 * 1024


def make_perm(move):
    pairs = []
    for source in range(128):
        place = np.unravel_index(source, SHAPE)
        target = [int(a) % b for a, b in zip(move(*place), SHAPE)]
        pairs.append((source, int(np.ravel_multi_index(target, SHAPE))))
    return pairs


X_UP = make_perm(lambda yh, x, z, yl, c: (yh, x + 1, z, yl, c))
X_DOWN = make_perm(lambda yh, x, z, yl, c: (yh, x - 1, z, yl, c))
Z_UP = make_perm(lambda yh, x, z, yl, c: (yh, x, z + 1, yl, c))
Z_DOWN = make_perm(lambda yh, x, z, yl, c: (yh, x, z - 1, yl, c))
Z_FAR = make_perm(lambda yh, x, z, yl, c: (yh, x, z + 2, yl, c))
X_FAR = make_perm(lambda yh, x, z, yl, c: (yh, x + 2, z, yl, c))
Y_HI = make_perm(lambda yh, x, z, yl, c: (yh + 1, x, z, yl, c))
Y_LO = make_perm(lambda yh, x, z, yl, c: (yh, x, z, yl + 1, c))
CORE = make_perm(lambda yh, x, z, yl, c: (yh, x, z, yl, c + 1))


def move(array, perm):
    return lax.ppermute(array, ("y_hi", "x", "grid"), perm)


def place():
    grid = lax.axis_index("grid")
    return (
        lax.axis_index("y_hi"),
        lax.axis_index("x"),
        grid // 4,
        (grid // 2) % 2,
        grid % 2,
    )


def cost(flops, bytes_accessed, transcendentals=0):
    return pl.CostEstimate(
        flops=flops, bytes_accessed=bytes_accessed, transcendentals=transcendentals
    )


def dot(a, b, ca, cb):
    return lax.dot_general(a, b, (((ca,), (cb,)), ((), ())), preferred_element_type=jnp.float32)


def attention_kernel(q_ref, k_ref, v_ref, o_ref, do_ref, out_ref):
    block = 256
    scale = 1.0 / math.sqrt(HEAD_DIM)
    rows = lax.broadcasted_iota(jnp.int32, (block, block), 0)
    cols = lax.broadcasted_iota(jnp.int32, (block, block), 1)
    keep = cols <= rows
    for r in range(SEQ_LEN // block):
        start, length = r * block, (r + 1) * block
        q = q_ref[start:length, :]
        do = do_ref[start:length, :]
        o = o_ref[start:length, :]
        delta = jnp.sum(do.astype(jnp.float32) * o.astype(jnp.float32), axis=-1, keepdims=True)
        diag = jnp.where(keep, dot(q, k_ref[start:length, :], 1, 1), -jnp.inf)
        row_max = jnp.max(diag, axis=-1, keepdims=True)
        if r:
            body = dot(q, k_ref[:start, :], 1, 1)
            row_max = jnp.maximum(row_max, jnp.max(body, axis=-1, keepdims=True))
        e = jnp.exp((diag - row_max) * scale)
        total = jnp.sum(e, axis=-1, keepdims=True)
        g = (e * (dot(do, v_ref[start:length, :], 1, 1) - delta)).astype(jnp.bfloat16)
        grad = dot(g, k_ref[start:length, :], 1, 0)
        if r:
            e = jnp.exp((body - row_max) * scale)
            total = total + jnp.sum(e, axis=-1, keepdims=True)
            g = (e * (dot(do, v_ref[:start, :], 1, 1) - delta)).astype(jnp.bfloat16)
            grad = grad + dot(g, k_ref[:start, :], 1, 0)
        grad = grad * (scale / total)
        out_ref[:, start:length] = grad.T.astype(jnp.bfloat16)


def attention(queries, keys, values, attn_out, grad_out, kv_index):
    heads = queries.shape[1] // HEAD_DIM
    mine = pl.BlockSpec((SEQ_LEN, HEAD_DIM), lambda h, kv: (0, h))
    shared = pl.BlockSpec((SEQ_LEN, HEAD_DIM), lambda h, kv: (0, kv[0]))

    def body(kv, *refs):
        attention_kernel(*refs)

    return pl.pallas_call(
        body,
        grid_spec=pltpu.PrefetchScalarGridSpec(
            num_scalar_prefetch=1,
            grid=(heads,),
            in_specs=[mine, shared, shared, mine, mine],
            out_specs=pl.BlockSpec((HEAD_DIM, SEQ_LEN), lambda h, kv: (h, 0)),
        ),
        out_shape=jax.ShapeDtypeStruct((heads * HEAD_DIM, SEQ_LEN), jnp.bfloat16),
        compiler_params=pltpu.CompilerParams(vmem_limit_bytes=VMEM),
        cost_estimate=cost(24 * 10**9, 8 * 10**6, 4 * 10**6),
        name="attention",
    )(kv_index, queries, keys, values, attn_out, grad_out)


def gradient_kernel(block_ref, gq_ref, in_ref, out_ref):
    out_ref[0] = dot(gq_ref[...], in_ref[...], 1, 0).astype(jnp.bfloat16)


def gradient_partial(grad_query_t, inputs, yh):
    return pl.pallas_call(
        gradient_kernel,
        grid_spec=pltpu.PrefetchScalarGridSpec(
            num_scalar_prefetch=1,
            grid=(4,),
            in_specs=[
                pl.BlockSpec((COLS, SEQ_LEN), lambda k, yh: (0, 0)),
                pl.BlockSpec((SEQ_LEN, ROWS), lambda k, yh: (0, yh[0] * 4 + k)),
            ],
            out_specs=pl.BlockSpec((1, COLS, ROWS), lambda k, yh: (k, 0, 0)),
        ),
        out_shape=jax.ShapeDtypeStruct((4, COLS, ROWS), jnp.bfloat16),
        compiler_params=pltpu.CompilerParams(vmem_limit_bytes=VMEM),
        cost_estimate=cost(16 * ROWS * COLS * SEQ_LEN, 12 * 10**6),
        name="gradient",
    )(yh.astype(jnp.int32).reshape(1), grad_query_t, inputs)


def momentum_kernel(m_ref, g_ref, h_ref, out_ref):
    total = h_ref[...].astype(jnp.float32)
    for n in range(4):
        total = total + g_ref[n].astype(jnp.float32)
    out_ref[...] = 0.95 * m_ref[...] + total.T


def momentum_of(momentum, terms, term):
    mine = pl.BlockSpec((128, COLS), lambda k: (k, 0))
    return pl.pallas_call(
        momentum_kernel,
        grid=(ROWS // 128,),
        in_specs=[
            mine,
            pl.BlockSpec((4, COLS, 128), lambda k: (0, 0, k)),
            pl.BlockSpec((COLS, 128), lambda k: (0, k)),
        ],
        out_specs=mine,
        out_shape=jax.ShapeDtypeStruct((ROWS, COLS), jnp.float32),
        compiler_params=pltpu.CompilerParams(vmem_limit_bytes=VMEM),
        cost_estimate=cost(9 * ROWS * COLS, 9 * 10**6),
        name="momentum",
    )(momentum, terms, term)


def gram_kernel(*refs):
    own, own_other = refs[8:10]
    outs, (lhs, rhs, sems) = refs[10:14], refs[14:]
    _, x, z, _, core = place()
    copies = []
    for n, block in enumerate(refs[:8]):
        slot = (x + n % 4 - z + 4) % 4
        side = slice(n // 4 * COLS, (n // 4 + 1) * COLS)
        copies.append(pltpu.make_async_copy(block, rhs.at[rows_of(slot, ROWS), side], sems.at[n]))
    for n, block in enumerate((own, own_other)):
        copies.append(
            pltpu.make_async_copy(
                block.at[rows_of(core, HALF), :],
                lhs.at[:, n * COLS : (n + 1) * COLS],
                sems.at[8 + n],
            )
        )
    for copy in copies:
        copy.start()
    for copy in copies:
        copy.wait()
    for pair in range(2):
        value = dot(lhs[...], rhs[pair * 2 * ROWS : (pair + 1) * 2 * ROWS, :], 1, 1)
        for n in range(2):
            out_ref = outs[pair * 2 + n]
            out_ref[...] = value[:, n * ROWS : (n + 1) * ROWS].astype(out_ref.dtype)


def gram_partial(own, own_other, blocks, other_blocks):
    shape = (HALF, ROWS)
    return pl.pallas_call(
        gram_kernel,
        in_specs=[pl.BlockSpec(memory_space=pl.ANY)] * 10,
        out_specs=[pl.BlockSpec(memory_space=pltpu.VMEM)] * 4,
        out_shape=[jax.ShapeDtypeStruct(shape, jnp.float32)]
        + [jax.ShapeDtypeStruct(shape, jnp.bfloat16)] * 3,
        scratch_shapes=[
            pltpu.VMEM((HALF, 2 * COLS), jnp.bfloat16),
            pltpu.VMEM((4 * ROWS, 2 * COLS), jnp.bfloat16),
            pltpu.SemaphoreType.DMA((10,)),
        ],
        compiler_params=pltpu.CompilerParams(vmem_limit_bytes=VMEM),
        cost_estimate=cost(1, 1),
        name="gram",
    )(*blocks, *other_blocks, own, own_other)


def piece_place(n):
    yh, x, z, yl, _ = place()
    return ((yl + n // 4 + yh) % 2) * 4 + (z + n % 4 - x + 4) % 4


def dp_block(n):
    yh, x, _, _, _ = place()
    return ((yh + n // 4) % 2) * 4 + (x + n % 4) % 4


def rows_of(index, size):
    return pl.ds(pl.multiple_of(index * size, size), size)


def square_kernel(*refs):
    grid_refs, dp_refs = refs[:8], refs[8:16]
    out_ref, lhs, rhs, acc, lhs_sems, rhs_sems = refs[20:]
    core = place()[4]
    dp_refs += tuple(refs[16].at[n] for n in range(5)) + refs[17:20]
    copies = []
    for n, piece in enumerate(grid_refs):
        copies.append(
            pltpu.make_async_copy(piece, lhs.at[:, rows_of(piece_place(n), ROWS)], lhs_sems.at[n])
        )
    for n, piece in enumerate(dp_refs):
        side = core if n < 8 else 1 - core
        copies.append(
            pltpu.make_async_copy(
                piece, rhs.at[rows_of(n % 8 * 2 + side, HALF), :], rhs_sems.at[n]
            )
        )
    for copy in copies:
        copy.start()
    for copy in copies[:8]:
        copy.wait()
    for k in range(4):
        for n in (2 * k, 2 * k + 1, 2 * k + 8, 2 * k + 9):
            copies[8 + n].wait()
        at = slice(k * 2 * ROWS, (k + 1) * 2 * ROWS)
        term = dot(lhs[:, at], rhs[at, :], 1, 0)
        if k:
            acc[...] += term
        else:
            acc[...] = term
    out = cubic_coef * lhs[:, rows_of(piece_place(0), ROWS)].astype(jnp.float32)
    out_ref[...] = (out + quintic_coef * acc[...]).astype(jnp.bfloat16)


def square(over_grid, over_dp):
    return pl.pallas_call(
        square_kernel,
        in_specs=[pl.BlockSpec(memory_space=pl.ANY)] * 20,
        out_specs=pl.BlockSpec(memory_space=pltpu.VMEM),
        out_shape=jax.ShapeDtypeStruct((HALF, ROWS), jnp.bfloat16),
        scratch_shapes=[
            pltpu.VMEM((HALF, D), jnp.bfloat16),
            pltpu.VMEM((D, ROWS), jnp.bfloat16),
            pltpu.VMEM((HALF, ROWS), jnp.float32),
            pltpu.SemaphoreType.DMA((8,)),
            pltpu.SemaphoreType.DMA((16,)),
        ],
        compiler_params=pltpu.CompilerParams(vmem_limit_bytes=VMEM),
        cost_estimate=cost(4 * HALF * D * ROWS, 11 * 10**6),
        name="square",
    )(*over_grid, *over_dp)


def update_kernel(*refs):
    n_refs, x_refs = refs[:8], refs[8:24]
    mine_ref, other_ref, lhs, rhs, acc, lhs_sems, rhs_sems = refs[24:]
    core = place()[4]
    copies = []
    for n, piece in enumerate(n_refs):
        copies.append(
            pltpu.make_async_copy(piece, lhs.at[:, rows_of(piece_place(n), ROWS)], lhs_sems.at[n])
        )
    for n in range(8):
        for side in range(2):
            copies.append(
                pltpu.make_async_copy(
                    x_refs[side * 8 + n],
                    rhs.at[n * ROWS : (n + 1) * ROWS, side * COLS : (side + 1) * COLS],
                    rhs_sems.at[2 * n + side],
                )
            )
    for copy in copies:
        copy.start()
    for copy in copies[:8]:
        copy.wait()
    for k in range(4):
        for copy in copies[8 + 4 * k : 12 + 4 * k]:
            copy.wait()
        at = slice(k * 2 * ROWS, (k + 1) * 2 * ROWS)
        term = dot(lhs[:, at], rhs[at, :], 1, 0)
        if k:
            acc[...] += term
        else:
            acc[...] = term
    own = rhs[rows_of(core, HALF), :].astype(jnp.float32)
    out = (math.sqrt(QD) * (linear_coef * own + acc[...])).astype(jnp.bfloat16)
    mine_ref[...] = out[:, :COLS]
    other_ref[...] = out[:, COLS:]


def update_of(pieces, blocks, other_blocks):
    inside = pl.BlockSpec(memory_space=pltpu.VMEM)
    out = jax.ShapeDtypeStruct((HALF, COLS), jnp.bfloat16)
    return pl.pallas_call(
        update_kernel,
        in_specs=[pl.BlockSpec(memory_space=pl.ANY)] * 24,
        out_specs=[inside, inside],
        out_shape=[out, out],
        scratch_shapes=[
            pltpu.VMEM((HALF, D), jnp.bfloat16),
            pltpu.VMEM((D, 2 * COLS), jnp.bfloat16),
            pltpu.VMEM((HALF, 2 * COLS), jnp.float32),
            pltpu.SemaphoreType.DMA((8,)),
            pltpu.SemaphoreType.DMA((16,)),
        ],
        compiler_params=pltpu.CompilerParams(vmem_limit_bytes=VMEM),
        cost_estimate=cost(1, 1),
        name="update",
    )(*pieces, *blocks, *other_blocks)


def per_device(inputs, queries, key_rows, values, attn_out, grad_out, momentum, iterate):
    yh, _, _, yl, core = place()
    together = lax.optimization_barrier
    f32, bf16 = jnp.float32, jnp.bfloat16

    own = iterate
    below = move(own, X_UP)
    above = move(own, X_DOWN)
    across = move(own, Y_HI)
    kv_index = (lax.axis_index("grid") // 2).astype(jnp.int32).reshape(1)
    grad_query_t = attention(queries, key_rows, values, attn_out, grad_out, kv_index)
    below, above, across, grad_query_t = together((below, above, across, grad_query_t))

    far_top, far_bottom = move(below[:HALF], X_UP), move(above[HALF:], X_DOWN)
    own_other, above_other, below_other = move(own, CORE), move(above, CORE), move(below, CORE)
    far_partial = gradient_partial(grad_query_t, inputs, 1 - yh)
    far_top, far_bottom, above, across, grad_query_t, far_partial = together(
        (far_top, far_bottom, above, across, grad_query_t, far_partial)
    )
    own_other, above_other, below_other, far_top = together(
        (own_other, above_other, below_other, far_top)
    )
    far = jnp.concatenate([far_top, far_bottom])

    across_below = move(across, X_UP)
    across_above = move(across, X_DOWN)
    across_far = move(far, Y_HI)
    far_other, across_other = move(far, CORE), move(across, CORE)
    near, near1, near2, near3 = gram_partial(
        own,
        own_other,
        (own, above, far, below),
        (own_other, above_other, far_other, below_other),
    )
    near1, near3 = move(near1, Z_UP), move(near3, Z_DOWN)
    partial = gradient_partial(grad_query_t, inputs, yh)
    across_below, across_above, across_far, across_other, near, near1, near2, near3, partial = (
        together(
            (across_below, across_above, across_far, across_other)
            + (near, near1, near2, near3, partial)
        )
    )
    far_partial, across_below = together((far_partial, across_below))
    far_terms = lax.all_to_all(far_partial, "x", 0, 0, tiled=True)

    far_swapped = move(across_far, CORE)
    above_swapped = move(across_above, CORE)
    below_swapped = move(across_below, CORE)
    near2 = move(near2, Z_FAR)
    far_swapped, above_swapped, below_swapped = together(
        (far_swapped, above_swapped, below_swapped)
    )
    other, other1, other2, other3 = gram_partial(
        own,
        own_other,
        (across, across_above, across_far, across_below),
        (across_other, above_swapped, far_swapped, below_swapped),
    )
    other, other1, other2, other3, near2 = together((other, other1, other2, other3, near2))
    other1, other2, other3 = move(other1, Z_UP), move(other2, Z_FAR), move(other3, Z_DOWN)
    near = near + near1.astype(f32) + near3.astype(f32) + near2.astype(f32)
    other1, other2, other3, near = together((other1, other2, other3, near))
    other = other + other1.astype(f32) + other3.astype(f32) + other2.astype(f32)
    same = yh == yl
    kept = jnp.where(same, near, other)
    rows = (kept + move(jnp.where(same, other, near).astype(bf16), Y_LO).astype(f32)).astype(bf16)

    rows, far_terms = together((rows, far_terms))

    z_below, z_above = move(rows, Z_UP), move(rows, Z_DOWN)
    x_below, x_above = move(rows, X_UP), move(rows, X_DOWN)
    lo, x_across = move(rows, Y_LO), move(rows, Y_HI)
    z_far, x_far = move(rows, Z_FAR), move(rows, X_FAR)
    z_below, z_above, x_below, x_above, lo, x_across, z_far, x_far = together(
        (z_below, z_above, x_below, x_above, lo, x_across, z_far, x_far)
    )
    lo_below, lo_above, lo_far = move(lo, Z_UP), move(lo, Z_DOWN), move(z_far, Y_LO)
    a_below, a_above, a_far = move(x_across, X_UP), move(x_across, X_DOWN), move(x_far, Y_HI)
    first_other = move(jnp.stack([rows, x_above, x_far, x_below, x_across]), CORE)
    lo_below, lo_above, lo_far, a_below, a_above, a_far = together(
        (lo_below, lo_above, lo_far, a_below, a_above, a_far)
    )
    partial, lo_below = together((partial, lo_below))
    terms = lax.all_to_all(partial, "x", 0, 0, tiled=True)
    combined = square(
        (rows, z_above, z_far, z_below, lo, lo_above, lo_far, lo_below),
        (rows, x_above, x_far, x_below, x_across, a_above, a_far, a_below)
        + (first_other, move(a_above, CORE), move(a_far, CORE), move(a_below, CORE)),
    )

    z_below, z_above = move(combined, Z_UP), move(combined, Z_DOWN)
    lo, z_far = move(combined, Y_LO), move(combined, Z_FAR)
    far_term = move(sum(far_terms[n].astype(f32) for n in range(4)).astype(bf16), Y_HI)
    z_below, z_above, lo, z_far, far_term = together((z_below, z_above, lo, z_far, far_term))
    lo_below, lo_above, lo_far = move(lo, Z_UP), move(lo, Z_DOWN), move(z_far, Y_LO)
    lo_below, lo_above, lo_far = together((lo_below, lo_above, lo_far))
    mine, theirs = update_of(
        (combined, z_above, z_far, z_below, lo, lo_above, lo_far, lo_below),
        (own, above, far, below, across, across_above, across_far, across_below),
        (own_other, above_other, far_other, below_other, across_other)
        + (above_swapped, far_swapped, below_swapped),
    )
    momentum, theirs = together((momentum, theirs))
    momentum_next = momentum_of(momentum, terms, far_term)
    theirs = move(theirs, CORE)
    update = jnp.where(
        core == 0, jnp.concatenate([mine, theirs]), jnp.concatenate([theirs, mine])
    )
    return (momentum_next, update)


def solution(mesh):
    parts = jax.sharding.Mesh(mesh.devices.reshape(2, 4, 16), ("y_hi", "x", "grid"))
    dp = ("y_hi", "x")
    rows, both = P(dp, None), P(dp, "grid")
    return jax.shard_map(
        per_device,
        mesh=parts,
        in_specs=(rows, both, rows, rows, both, both, both, both),
        out_specs=(both, both),
        check_vma=False,
    )
```

```python
import math

import jax
import jax.numpy as jnp
import numpy as np
from jax import lax
from jax.experimental import pallas as pl
from jax.experimental.pallas import tpu as pltpu
from jax.sharding import PartitionSpec as P

HEADS = 96
KV_HEADS = 8
HEAD_DIM = 128
SEQ_LEN = 1024
QD = 12288
D = 5120
ROWS = 640
COLS = 768
HALF = 320
QUART = 160
SHAPE = (2, 4, 4, 2, 2)

linear_coef = 3.4445
cubic_coef = -4.775
quintic_coef = 2.0315

VMEM = 60 * 1024 * 1024


def make_perm(move):
    pairs = []
    for source in range(128):
        place = np.unravel_index(source, SHAPE)
        target = [int(a) % b for a, b in zip(move(*place), SHAPE)]
        pairs.append((source, int(np.ravel_multi_index(target, SHAPE))))
    return pairs


X_UP = make_perm(lambda yh, x, z, yl, c: (yh, x + 1, z, yl, c))
X_DOWN = make_perm(lambda yh, x, z, yl, c: (yh, x - 1, z, yl, c))
Z_UP = make_perm(lambda yh, x, z, yl, c: (yh, x, z + 1, yl, c))
Z_DOWN = make_perm(lambda yh, x, z, yl, c: (yh, x, z - 1, yl, c))
Z_FAR = make_perm(lambda yh, x, z, yl, c: (yh, x, z + 2, yl, c))
X_FAR = make_perm(lambda yh, x, z, yl, c: (yh, x + 2, z, yl, c))
Y_HI = make_perm(lambda yh, x, z, yl, c: (yh + 1, x, z, yl, c))
Y_LO = make_perm(lambda yh, x, z, yl, c: (yh, x, z, yl + 1, c))
CORE = make_perm(lambda yh, x, z, yl, c: (yh, x, z, yl, c + 1))


def move(array, perm):
    return lax.ppermute(array, ("y_hi", "x", "grid"), perm)


def place():
    grid = lax.axis_index("grid")
    return (
        lax.axis_index("y_hi"),
        lax.axis_index("x"),
        grid // 4,
        (grid // 2) % 2,
        grid % 2,
    )


def cost(flops, bytes_accessed, transcendentals=0):
    return pl.CostEstimate(
        flops=flops, bytes_accessed=bytes_accessed, transcendentals=transcendentals
    )


def dot(a, b, ca, cb):
    return lax.dot_general(a, b, (((ca,), (cb,)), ((), ())), preferred_element_type=jnp.float32)


def attention_kernel(q_ref, k_ref, v_ref, o_ref, do_ref, out_ref):
    block = 256
    scale = 1.0 / math.sqrt(HEAD_DIM)
    rows = lax.broadcasted_iota(jnp.int32, (block, block), 0)
    cols = lax.broadcasted_iota(jnp.int32, (block, block), 1)
    keep = cols <= rows
    for r in range(SEQ_LEN // block):
        start, length = r * block, (r + 1) * block
        q = q_ref[start:length, :]
        do = do_ref[start:length, :]
        o = o_ref[start:length, :]
        delta = jnp.sum(do.astype(jnp.float32) * o.astype(jnp.float32), axis=-1, keepdims=True)
        diag = jnp.where(keep, dot(q, k_ref[start:length, :], 1, 1), -jnp.inf)
        row_max = jnp.max(diag, axis=-1, keepdims=True)
        if r:
            body = dot(q, k_ref[:start, :], 1, 1)
            row_max = jnp.maximum(row_max, jnp.max(body, axis=-1, keepdims=True))
        e = jnp.exp((diag - row_max) * scale)
        total = jnp.sum(e, axis=-1, keepdims=True)
        g = (e * (dot(do, v_ref[start:length, :], 1, 1) - delta)).astype(jnp.bfloat16)
        grad = dot(g, k_ref[start:length, :], 1, 0)
        if r:
            e = jnp.exp((body - row_max) * scale)
            total = total + jnp.sum(e, axis=-1, keepdims=True)
            g = (e * (dot(do, v_ref[:start, :], 1, 1) - delta)).astype(jnp.bfloat16)
            grad = grad + dot(g, k_ref[:start, :], 1, 0)
        grad = grad * (scale / total)
        out_ref[:, start:length] = grad.T.astype(jnp.bfloat16)


def attention(queries, keys, values, attn_out, grad_out, kv_index):
    heads = queries.shape[1] // HEAD_DIM
    mine = pl.BlockSpec((SEQ_LEN, HEAD_DIM), lambda h, kv: (0, h))
    shared = pl.BlockSpec((SEQ_LEN, HEAD_DIM), lambda h, kv: (0, kv[0]))

    def body(kv, *refs):
        attention_kernel(*refs)

    return pl.pallas_call(
        body,
        grid_spec=pltpu.PrefetchScalarGridSpec(
            num_scalar_prefetch=1,
            grid=(heads,),
            in_specs=[mine, shared, shared, mine, mine],
            out_specs=pl.BlockSpec((HEAD_DIM, SEQ_LEN), lambda h, kv: (h, 0)),
        ),
        out_shape=jax.ShapeDtypeStruct((heads * HEAD_DIM, SEQ_LEN), jnp.bfloat16),
        compiler_params=pltpu.CompilerParams(vmem_limit_bytes=VMEM),
        cost_estimate=cost(24 * 10**9, 8 * 10**6, 4 * 10**6),
        name="attention",
    )(kv_index, queries, keys, values, attn_out, grad_out)


def gradient_kernel(block_ref, gq_ref, in_ref, out_ref):
    out_ref[0] = dot(gq_ref[...], in_ref[...], 1, 0).astype(jnp.bfloat16)


def gradient_partial(grad_query_t, inputs, yh):
    return pl.pallas_call(
        gradient_kernel,
        grid_spec=pltpu.PrefetchScalarGridSpec(
            num_scalar_prefetch=1,
            grid=(4,),
            in_specs=[
                pl.BlockSpec((COLS, SEQ_LEN), lambda k, yh: (0, 0)),
                pl.BlockSpec((SEQ_LEN, ROWS), lambda k, yh: (0, yh[0] * 4 + k)),
            ],
            out_specs=pl.BlockSpec((1, COLS, ROWS), lambda k, yh: (k, 0, 0)),
        ),
        out_shape=jax.ShapeDtypeStruct((4, COLS, ROWS), jnp.bfloat16),
        compiler_params=pltpu.CompilerParams(vmem_limit_bytes=VMEM),
        cost_estimate=cost(16 * ROWS * COLS * SEQ_LEN, 12 * 10**6),
        name="gradient",
    )(yh.astype(jnp.int32).reshape(1), grad_query_t, inputs)


def momentum_kernel(m_ref, g_ref, h_ref, out_ref):
    total = h_ref[...].astype(jnp.float32)
    for n in range(4):
        total = total + g_ref[n].astype(jnp.float32)
    out_ref[...] = 0.95 * m_ref[...] + total.T


def momentum_of(momentum, terms, term):
    mine = pl.BlockSpec((128, COLS), lambda k: (k, 0))
    return pl.pallas_call(
        momentum_kernel,
        grid=(ROWS // 128,),
        in_specs=[
            mine,
            pl.BlockSpec((4, COLS, 128), lambda k: (0, 0, k)),
            pl.BlockSpec((COLS, 128), lambda k: (0, k)),
        ],
        out_specs=mine,
        out_shape=jax.ShapeDtypeStruct((ROWS, COLS), jnp.float32),
        compiler_params=pltpu.CompilerParams(vmem_limit_bytes=VMEM),
        cost_estimate=cost(9 * ROWS * COLS, 9 * 10**6),
        name="momentum",
    )(momentum, terms, term)


def gram_kernel(*refs):
    own, own_other = refs[8:10]
    outs, (lhs, rhs, sems) = refs[10:14], refs[14:]
    _, x, z, _, core = place()
    copies = []
    for n, block in enumerate(refs[:8]):
        slot = (x + n % 4 - z + 4) % 4
        side = slice(n // 4 * COLS, (n // 4 + 1) * COLS)
        copies.append(pltpu.make_async_copy(block, rhs.at[rows_of(slot, ROWS), side], sems.at[n]))
    for n, block in enumerate((own, own_other)):
        copies.append(
            pltpu.make_async_copy(
                block.at[rows_of(core, HALF), :],
                lhs.at[:, n * COLS : (n + 1) * COLS],
                sems.at[8 + n],
            )
        )
    for copy in copies:
        copy.start()
    for copy in copies:
        copy.wait()
    for pair in range(2):
        value = dot(lhs[...], rhs[pair * 2 * ROWS : (pair + 1) * 2 * ROWS, :], 1, 1)
        for n in range(2):
            out_ref = outs[pair * 2 + n]
            out_ref[...] = value[:, n * ROWS : (n + 1) * ROWS].astype(out_ref.dtype)


def gram_partial(own, own_other, blocks, other_blocks):
    shape = (HALF, ROWS)
    return pl.pallas_call(
        gram_kernel,
        in_specs=[pl.BlockSpec(memory_space=pl.ANY)] * 10,
        out_specs=[pl.BlockSpec(memory_space=pltpu.VMEM)] * 4,
        out_shape=[jax.ShapeDtypeStruct(shape, jnp.float32)]
        + [jax.ShapeDtypeStruct(shape, jnp.bfloat16)] * 3,
        scratch_shapes=[
            pltpu.VMEM((HALF, 2 * COLS), jnp.bfloat16),
            pltpu.VMEM((4 * ROWS, 2 * COLS), jnp.bfloat16),
            pltpu.SemaphoreType.DMA((10,)),
        ],
        compiler_params=pltpu.CompilerParams(vmem_limit_bytes=VMEM),
        cost_estimate=cost(1, 1),
        name="gram",
    )(*blocks, *other_blocks, own, own_other)


def piece_place(n):
    yh, x, z, yl, _ = place()
    return ((yl + n // 4 + yh) % 2) * 4 + (z + n % 4 - x + 4) % 4


def dp_block(n):
    yh, x, _, _, _ = place()
    return ((yh + n // 4) % 2) * 4 + (x + n % 4) % 4


def rows_of(index, size):
    return pl.ds(pl.multiple_of(index * size, size), size)


def square_kernel(*refs):
    grid_refs, dp_refs = refs[:8], refs[8:12]
    out_ref, lhs, rhs, acc, lhs_sems, rhs_sems = refs[12:]
    yh, _, z, yl, core = place()
    places = [((yl + n // 4 + yh) % 2) * 4 + (z + n % 4) % 4 for n in range(8)]
    copies = []
    for n, piece in enumerate(grid_refs):
        copies.append(
            pltpu.make_async_copy(piece, lhs.at[:, rows_of(places[n], ROWS)], lhs_sems.at[n])
        )
    for n in range(16):
        side = core if n < 8 else 1 - core
        copies.append(
            pltpu.make_async_copy(
                dp_refs[n // 4].at[n % 4],
                rhs.at[rows_of(n % 8 * 2 + side, HALF), :],
                rhs_sems.at[n],
            )
        )
    for copy in copies:
        copy.start()
    for copy in copies[:8]:
        copy.wait()
    for k in range(4):
        for n in (2 * k, 2 * k + 1, 2 * k + 8, 2 * k + 9):
            copies[8 + n].wait()
        at = slice(k * 2 * ROWS, (k + 1) * 2 * ROWS)
        term = dot(lhs[:, at], rhs[at, :], 1, 0)
        if k:
            acc[...] += term
        else:
            acc[...] = term
    out = cubic_coef * lhs[:, rows_of(places[0], ROWS)].astype(jnp.float32)
    out_ref[...] = (out + quintic_coef * acc[...]).astype(jnp.bfloat16)


def square(over_grid, over_dp):
    return pl.pallas_call(
        square_kernel,
        in_specs=[pl.BlockSpec(memory_space=pl.ANY)] * 12,
        out_specs=pl.BlockSpec(memory_space=pltpu.VMEM),
        out_shape=jax.ShapeDtypeStruct((HALF, ROWS), jnp.bfloat16),
        scratch_shapes=[
            pltpu.VMEM((HALF, D), jnp.bfloat16),
            pltpu.VMEM((D, ROWS), jnp.bfloat16),
            pltpu.VMEM((HALF, ROWS), jnp.float32),
            pltpu.SemaphoreType.DMA((8,)),
            pltpu.SemaphoreType.DMA((16,)),
        ],
        compiler_params=pltpu.CompilerParams(vmem_limit_bytes=VMEM),
        cost_estimate=cost(4 * HALF * D * ROWS, 11 * 10**6),
        name="square",
    )(*over_grid, *over_dp)


def update_kernel(*refs):
    n_refs, x_refs = refs[:8], refs[8:24]
    mine_ref, other_ref, lhs, rhs, acc, lhs_sems, rhs_sems = refs[24:]
    core = place()[4]
    copies = []
    for n, piece in enumerate(n_refs):
        copies.append(
            pltpu.make_async_copy(piece, lhs.at[:, rows_of(piece_place(n), ROWS)], lhs_sems.at[n])
        )
    for n in range(8):
        for side in range(2):
            copies.append(
                pltpu.make_async_copy(
                    x_refs[side * 8 + n],
                    rhs.at[n * ROWS : (n + 1) * ROWS, side * COLS : (side + 1) * COLS],
                    rhs_sems.at[2 * n + side],
                )
            )
    for copy in copies:
        copy.start()
    for copy in copies[:8]:
        copy.wait()
    for k in range(4):
        for copy in copies[8 + 4 * k : 12 + 4 * k]:
            copy.wait()
        at = slice(k * 2 * ROWS, (k + 1) * 2 * ROWS)
        term = dot(lhs[:, at], rhs[at, :], 1, 0)
        if k:
            acc[...] += term
        else:
            acc[...] = term
    own = rhs[rows_of(core, HALF), :].astype(jnp.float32)
    out = (math.sqrt(QD) * (linear_coef * own + acc[...])).astype(jnp.bfloat16)
    mine_ref[rows_of(core, HALF), :] = out[:, :COLS]
    other_ref[...] = out[:, COLS:]


def update_of(pieces, blocks, other_blocks):
    inside = pl.BlockSpec(memory_space=pltpu.VMEM)
    mine = jax.ShapeDtypeStruct((ROWS, COLS), jnp.bfloat16)
    other = jax.ShapeDtypeStruct((HALF, COLS), jnp.bfloat16)
    return pl.pallas_call(
        update_kernel,
        in_specs=[pl.BlockSpec(memory_space=pl.ANY)] * 24,
        out_specs=[inside, inside],
        out_shape=[mine, other],
        scratch_shapes=[
            pltpu.VMEM((HALF, D), jnp.bfloat16),
            pltpu.VMEM((D, 2 * COLS), jnp.bfloat16),
            pltpu.VMEM((HALF, 2 * COLS), jnp.float32),
            pltpu.SemaphoreType.DMA((8,)),
            pltpu.SemaphoreType.DMA((16,)),
        ],
        compiler_params=pltpu.CompilerParams(vmem_limit_bytes=VMEM),
        cost_estimate=cost(1, 1),
        name="update",
    )(*pieces, *blocks, *other_blocks)


def per_device(inputs, queries, key_rows, values, attn_out, grad_out, momentum, iterate):
    yh, _, _, yl, core = place()
    together = lax.optimization_barrier
    f32, bf16 = jnp.float32, jnp.bfloat16

    own = iterate
    below = move(own, X_UP)
    above = move(own, X_DOWN)
    across = move(own, Y_HI)
    kv_index = (lax.axis_index("grid") // 2).astype(jnp.int32).reshape(1)
    grad_query_t = attention(queries, key_rows, values, attn_out, grad_out, kv_index)
    below, above, across, grad_query_t = together((below, above, across, grad_query_t))

    far_top, far_bottom = move(below[:HALF], X_UP), move(above[HALF:], X_DOWN)
    own_other, above_other, below_other = move(own, CORE), move(above, CORE), move(below, CORE)
    far_partial = gradient_partial(grad_query_t, inputs, 1 - yh)
    far_top, far_bottom, above, across, grad_query_t, far_partial = together(
        (far_top, far_bottom, above, across, grad_query_t, far_partial)
    )
    own_other, above_other, below_other, far_top = together(
        (own_other, above_other, below_other, far_top)
    )
    far = jnp.concatenate([far_top, far_bottom])

    across_below = move(across, X_UP)
    across_above = move(across, X_DOWN)
    across_far = move(far, Y_HI)
    far_other, across_other = move(far, CORE), move(across, CORE)
    near, near1, near2, near3 = gram_partial(
        own,
        own_other,
        (own, above, far, below),
        (own_other, above_other, far_other, below_other),
    )
    far_partial, near = together((far_partial, near))
    far_terms = lax.all_to_all(far_partial, "x", 0, 0, tiled=True)
    near1, near3 = move(near1, Z_UP), move(near3, Z_DOWN)
    across_below, across_above, across_far, across_other, near, near1, near2, near3 = together(
        (across_below, across_above, across_far, across_other, near, near1, near2, near3)
    )

    far_swapped = move(across_far, CORE)
    above_swapped = move(across_above, CORE)
    below_swapped = move(across_below, CORE)
    near2 = move(near2, Z_FAR)
    far_swapped, above_swapped, below_swapped = together(
        (far_swapped, above_swapped, below_swapped)
    )
    other, other1, other2, other3 = gram_partial(
        own,
        own_other,
        (across, across_above, across_far, across_below),
        (across_other, above_swapped, far_swapped, below_swapped),
    )
    other, other1, other2, other3, near2 = together((other, other1, other2, other3, near2))
    other1, other2, other3 = move(other1, Z_UP), move(other2, Z_FAR), move(other3, Z_DOWN)
    near = near + near1.astype(f32) + near3.astype(f32) + near2.astype(f32)
    other1, other2, other3, near = together((other1, other2, other3, near))
    other = other + other1.astype(f32) + other3.astype(f32) + other2.astype(f32)
    same = yh == yl
    kept = jnp.where(same, near, other)
    rows = (kept + move(jnp.where(same, other, near).astype(bf16), Y_LO).astype(f32)).astype(bf16)

    rows, far_terms, grad_query_t = together((rows, far_terms, grad_query_t))

    def along_x(piece):
        return lax.all_to_all(jnp.broadcast_to(piece, (4, HALF, ROWS)), "x", 0, 0, tiled=True)

    lo, z_far = move(rows, Y_LO), move(rows, Z_FAR)
    across_rows = move(rows, Y_HI)
    here = along_x(rows)
    partial = gradient_partial(grad_query_t, inputs, yh)
    far_term = sum(far_terms[n].astype(f32) for n in range(4)).astype(bf16)
    rows, lo, z_far, across_rows, here, partial, far_term = together(
        (rows, lo, z_far, across_rows, here, partial, far_term)
    )
    z_below, z_above = move(rows, Z_UP), move(rows, Z_DOWN)
    lo_below, lo_above, lo_far = move(lo, Z_UP), move(lo, Z_DOWN), move(z_far, Y_LO)
    there = along_x(across_rows)
    partial, lo_below = together((partial, lo_below))
    terms = lax.all_to_all(partial, "x", 0, 0, tiled=True)
    z_below, z_above, lo_below, lo_above, lo_far, there, here, far_term = together(
        (z_below, z_above, lo_below, lo_above, lo_far, there, here, far_term)
    )
    combined = square(
        (rows, z_above, z_far, z_below, lo, lo_above, lo_far, lo_below),
        (here, there, move(here, CORE), move(there, CORE)),
    )

    z_below, z_above = move(combined, Z_UP), move(combined, Z_DOWN)
    lo, z_far = move(combined, Y_LO), move(combined, Z_FAR)
    far_term = move(far_term, Y_HI)
    z_below, z_above, lo, z_far, far_term = together((z_below, z_above, lo, z_far, far_term))
    lo_below, lo_above, lo_far = move(lo, Z_UP), move(lo, Z_DOWN), move(z_far, Y_LO)
    momentum_next = momentum_of(momentum, terms, far_term)
    lo_below, lo_above, lo_far, momentum_next = together(
        (lo_below, lo_above, lo_far, momentum_next)
    )
    mine, theirs = update_of(
        (combined, z_above, z_far, z_below, lo, lo_above, lo_far, lo_below),
        (own, above, far, below, across, across_above, across_far, across_below),
        (own_other, above_other, far_other, below_other, across_other)
        + (above_swapped, far_swapped, below_swapped),
    )
    update = lax.dynamic_update_slice(mine, move(theirs, CORE), ((1 - core) * HALF, 0))
    return (momentum_next, update)


def solution(mesh):
    parts = jax.sharding.Mesh(mesh.devices.reshape(2, 4, 16), ("y_hi", "x", "grid"))
    dp = ("y_hi", "x")
    rows, both = P(dp, None), P(dp, "grid")
    return jax.shard_map(
        per_device,
        mesh=parts,
        in_specs=(rows, both, rows, rows, both, both, both, both),
        out_specs=(both, both),
        check_vma=False,
    )
```

```python
import math

import jax
import jax.numpy as jnp
import numpy as np
from jax import lax
from jax.experimental import pallas as pl
from jax.experimental.pallas import tpu as pltpu
from jax.sharding import PartitionSpec as P

HEADS = 96
KV_HEADS = 8
HEAD_DIM = 128
SEQ_LEN = 1024
QD = 12288
D = 5120
ROWS = 640
COLS = 768
HALF = 320
QUART = 160
SHAPE = (2, 4, 4, 2, 2)

linear_coef = 3.4445
cubic_coef = -4.775
quintic_coef = 2.0315

VMEM = 60 * 1024 * 1024


def make_perm(move):
    pairs = []
    for source in range(128):
        place = np.unravel_index(source, SHAPE)
        target = [int(a) % b for a, b in zip(move(*place), SHAPE)]
        pairs.append((source, int(np.ravel_multi_index(target, SHAPE))))
    return pairs


X_UP = make_perm(lambda yh, x, z, yl, c: (yh, x + 1, z, yl, c))
X_DOWN = make_perm(lambda yh, x, z, yl, c: (yh, x - 1, z, yl, c))
Z_UP = make_perm(lambda yh, x, z, yl, c: (yh, x, z + 1, yl, c))
Z_DOWN = make_perm(lambda yh, x, z, yl, c: (yh, x, z - 1, yl, c))
Z_FAR = make_perm(lambda yh, x, z, yl, c: (yh, x, z + 2, yl, c))
X_FAR = make_perm(lambda yh, x, z, yl, c: (yh, x + 2, z, yl, c))
Y_HI = make_perm(lambda yh, x, z, yl, c: (yh + 1, x, z, yl, c))
Y_LO = make_perm(lambda yh, x, z, yl, c: (yh, x, z, yl + 1, c))
CORE = make_perm(lambda yh, x, z, yl, c: (yh, x, z, yl, c + 1))


def move(array, perm):
    return lax.ppermute(array, ("y_hi", "x", "grid"), perm)


def place():
    grid = lax.axis_index("grid")
    return (
        lax.axis_index("y_hi"),
        lax.axis_index("x"),
        grid // 4,
        (grid // 2) % 2,
        grid % 2,
    )


def cost(flops, bytes_accessed, transcendentals=0):
    return pl.CostEstimate(
        flops=flops, bytes_accessed=bytes_accessed, transcendentals=transcendentals
    )


def dot(a, b, ca, cb):
    return lax.dot_general(a, b, (((ca,), (cb,)), ((), ())), preferred_element_type=jnp.float32)


def attention_kernel(q_ref, k_ref, v_ref, o_ref, do_ref, out_ref):
    block = 256
    scale = 1.0 / math.sqrt(HEAD_DIM)
    rows = lax.broadcasted_iota(jnp.int32, (block, block), 0)
    cols = lax.broadcasted_iota(jnp.int32, (block, block), 1)
    keep = cols <= rows
    for r in range(SEQ_LEN // block):
        start, length = r * block, (r + 1) * block
        q = q_ref[start:length, :]
        do = do_ref[start:length, :]
        o = o_ref[start:length, :]
        delta = jnp.sum(do.astype(jnp.float32) * o.astype(jnp.float32), axis=-1, keepdims=True)
        diag = jnp.where(keep, dot(q, k_ref[start:length, :], 1, 1), -jnp.inf)
        row_max = jnp.max(diag, axis=-1, keepdims=True)
        if r:
            body = dot(q, k_ref[:start, :], 1, 1)
            row_max = jnp.maximum(row_max, jnp.max(body, axis=-1, keepdims=True))
        e = jnp.exp((diag - row_max) * scale)
        total = jnp.sum(e, axis=-1, keepdims=True)
        g = (e * (dot(do, v_ref[start:length, :], 1, 1) - delta)).astype(jnp.bfloat16)
        grad = dot(g, k_ref[start:length, :], 1, 0)
        if r:
            e = jnp.exp((body - row_max) * scale)
            total = total + jnp.sum(e, axis=-1, keepdims=True)
            g = (e * (dot(do, v_ref[:start, :], 1, 1) - delta)).astype(jnp.bfloat16)
            grad = grad + dot(g, k_ref[:start, :], 1, 0)
        grad = grad * (scale / total)
        out_ref[:, start:length] = grad.T.astype(jnp.bfloat16)


def attention(queries, keys, values, attn_out, grad_out, kv_index):
    heads = queries.shape[1] // HEAD_DIM
    mine = pl.BlockSpec((SEQ_LEN, HEAD_DIM), lambda h, kv: (0, h))
    shared = pl.BlockSpec((SEQ_LEN, HEAD_DIM), lambda h, kv: (0, kv[0]))

    def body(kv, *refs):
        attention_kernel(*refs)

    return pl.pallas_call(
        body,
        grid_spec=pltpu.PrefetchScalarGridSpec(
            num_scalar_prefetch=1,
            grid=(heads,),
            in_specs=[mine, shared, shared, mine, mine],
            out_specs=pl.BlockSpec((HEAD_DIM, SEQ_LEN), lambda h, kv: (h, 0)),
        ),
        out_shape=jax.ShapeDtypeStruct((heads * HEAD_DIM, SEQ_LEN), jnp.bfloat16),
        compiler_params=pltpu.CompilerParams(vmem_limit_bytes=VMEM),
        cost_estimate=cost(24 * 10**9, 8 * 10**6, 4 * 10**6),
        name="attention",
    )(kv_index, queries, keys, values, attn_out, grad_out)


def gradient_kernel(block_ref, gq_ref, in_ref, out_ref):
    out_ref[0] = dot(gq_ref[...], in_ref[...], 1, 0).astype(jnp.bfloat16)


def gradient_partial(grad_query_t, inputs, yh):
    return pl.pallas_call(
        gradient_kernel,
        grid_spec=pltpu.PrefetchScalarGridSpec(
            num_scalar_prefetch=1,
            grid=(4,),
            in_specs=[
                pl.BlockSpec((COLS, SEQ_LEN), lambda k, yh: (0, 0)),
                pl.BlockSpec((SEQ_LEN, ROWS), lambda k, yh: (0, yh[0] * 4 + k)),
            ],
            out_specs=pl.BlockSpec((1, COLS, ROWS), lambda k, yh: (k, 0, 0)),
        ),
        out_shape=jax.ShapeDtypeStruct((4, COLS, ROWS), jnp.bfloat16),
        compiler_params=pltpu.CompilerParams(vmem_limit_bytes=VMEM),
        cost_estimate=cost(16 * ROWS * COLS * SEQ_LEN, 12 * 10**6),
        name="gradient",
    )(yh.astype(jnp.int32).reshape(1), grad_query_t, inputs)


def momentum_kernel(m_ref, g_ref, h_ref, out_ref):
    total = h_ref[...].astype(jnp.float32)
    for n in range(4):
        total = total + g_ref[n].astype(jnp.float32)
    out_ref[...] = 0.95 * m_ref[...] + total.T


def momentum_of(momentum, terms, term):
    mine = pl.BlockSpec((128, COLS), lambda k: (k, 0))
    return pl.pallas_call(
        momentum_kernel,
        grid=(ROWS // 128,),
        in_specs=[
            mine,
            pl.BlockSpec((4, COLS, 128), lambda k: (0, 0, k)),
            pl.BlockSpec((COLS, 128), lambda k: (0, k)),
        ],
        out_specs=mine,
        out_shape=jax.ShapeDtypeStruct((ROWS, COLS), jnp.float32),
        compiler_params=pltpu.CompilerParams(vmem_limit_bytes=VMEM),
        cost_estimate=cost(9 * ROWS * COLS, 9 * 10**6),
        name="momentum",
    )(momentum, terms, term)


def gram_kernel(*refs):
    own, own_other = refs[8:10]
    outs, (lhs, rhs, acc, sems) = refs[10:14], refs[14:]
    _, x, z, _, core = place()
    copies = ([], [])
    for n, block in enumerate((own, own_other)):
        source = block.at[rows_of(core, HALF), :]
        copies[n].append(
            pltpu.make_async_copy(source, lhs.at[:, n * COLS : (n + 1) * COLS], sems.at[8 + n])
        )
    for n, block in enumerate(refs[:8]):
        slot = (x + n % 4 - z + 4) % 4
        side = slice(n // 4 * COLS, (n // 4 + 1) * COLS)
        copies[n // 4].append(
            pltpu.make_async_copy(block, rhs.at[rows_of(slot, ROWS), side], sems.at[n])
        )
    for copy in copies[0]:
        copy.start()
    for copy in copies[0]:
        copy.wait()
    for copy in copies[1]:
        copy.start()
    pairs = [slice(pair * 2 * ROWS, (pair + 1) * 2 * ROWS) for pair in range(2)]
    for at in pairs:
        acc[:, at] = dot(lhs[:, :COLS], rhs[at, :COLS], 1, 1)
    for copy in copies[1]:
        copy.wait()
    for pair, at in enumerate(pairs):
        value = acc[:, at] + dot(lhs[:, COLS:], rhs[at, COLS:], 1, 1)
        for n in range(2):
            out_ref = outs[pair * 2 + n]
            out_ref[...] = value[:, n * ROWS : (n + 1) * ROWS].astype(out_ref.dtype)


def gram_partial(own, own_other, blocks, other_blocks):
    shape = (HALF, ROWS)
    return pl.pallas_call(
        gram_kernel,
        in_specs=[pl.BlockSpec(memory_space=pl.ANY)] * 10,
        out_specs=[pl.BlockSpec(memory_space=pltpu.VMEM)] * 4,
        out_shape=[jax.ShapeDtypeStruct(shape, jnp.float32)]
        + [jax.ShapeDtypeStruct(shape, jnp.bfloat16)] * 3,
        scratch_shapes=[
            pltpu.VMEM((HALF, 2 * COLS), jnp.bfloat16),
            pltpu.VMEM((4 * ROWS, 2 * COLS), jnp.bfloat16),
            pltpu.VMEM((HALF, 4 * ROWS), jnp.float32),
            pltpu.SemaphoreType.DMA((10,)),
        ],
        compiler_params=pltpu.CompilerParams(vmem_limit_bytes=VMEM),
        cost_estimate=cost(1, 1),
        name="gram",
    )(*blocks, *other_blocks, own, own_other)


def piece_place(n):
    yh, x, z, yl, _ = place()
    return ((yl + n // 4 + yh) % 2) * 4 + (z + n % 4 - x + 4) % 4


def dp_block(n):
    yh, x, _, _, _ = place()
    return ((yh + n // 4) % 2) * 4 + (x + n % 4) % 4


def rows_of(index, size):
    return pl.ds(pl.multiple_of(index * size, size), size)


def square_kernel(*refs):
    grid_refs, dp_refs = refs[:8], refs[8:12]
    out_ref, lhs, rhs, acc, lhs_sems, rhs_sems = refs[12:]
    yh, _, z, yl, core = place()
    places = [((yl + n // 4 + yh) % 2) * 4 + (z + n % 4) % 4 for n in range(8)]
    copies = []
    for n, piece in enumerate(grid_refs):
        copies.append(
            pltpu.make_async_copy(piece, lhs.at[:, rows_of(places[n], ROWS)], lhs_sems.at[n])
        )
    for n in range(16):
        side = core if n < 8 else 1 - core
        copies.append(
            pltpu.make_async_copy(
                dp_refs[n // 4].at[n % 4],
                rhs.at[rows_of(n % 8 * 2 + side, HALF), :],
                rhs_sems.at[n],
            )
        )
    chunks = [[copies[8 + n] for n in (2 * k, 2 * k + 1, 2 * k + 8, 2 * k + 9)] for k in range(4)]
    for copy in copies[:8] + chunks[0]:
        copy.start()
    for copy in copies[:8]:
        copy.wait()
    for k in range(4):
        for copy in chunks[k]:
            copy.wait()
        if k < 3:
            for copy in chunks[k + 1]:
                copy.start()
        at = slice(k * 2 * ROWS, (k + 1) * 2 * ROWS)
        term = dot(lhs[:, at], rhs[at, :], 1, 0)
        if k:
            acc[...] += term
        else:
            acc[...] = term
    out = cubic_coef * lhs[:, rows_of(places[0], ROWS)].astype(jnp.float32)
    out_ref[...] = (out + quintic_coef * acc[...]).astype(jnp.bfloat16)


def square(over_grid, over_dp):
    return pl.pallas_call(
        square_kernel,
        in_specs=[pl.BlockSpec(memory_space=pl.ANY)] * 12,
        out_specs=pl.BlockSpec(memory_space=pltpu.VMEM),
        out_shape=jax.ShapeDtypeStruct((HALF, ROWS), jnp.bfloat16),
        scratch_shapes=[
            pltpu.VMEM((HALF, D), jnp.bfloat16),
            pltpu.VMEM((D, ROWS), jnp.bfloat16),
            pltpu.VMEM((HALF, ROWS), jnp.float32),
            pltpu.SemaphoreType.DMA((8,)),
            pltpu.SemaphoreType.DMA((16,)),
        ],
        compiler_params=pltpu.CompilerParams(vmem_limit_bytes=VMEM),
        cost_estimate=cost(4 * HALF * D * ROWS, 11 * 10**6),
        name="square",
    )(*over_grid, *over_dp)


def update_kernel(*refs):
    n_refs, x_refs = refs[:8], refs[8:24]
    mine_ref, other_ref, lhs, rhs, acc, lhs_sems, rhs_sems = refs[24:]
    core = place()[4]
    copies = []
    for n, piece in enumerate(n_refs):
        copies.append(
            pltpu.make_async_copy(piece, lhs.at[:, rows_of(piece_place(n), ROWS)], lhs_sems.at[n])
        )
    for n in range(8):
        for side in range(2):
            copies.append(
                pltpu.make_async_copy(
                    x_refs[side * 8 + n],
                    rhs.at[n * ROWS : (n + 1) * ROWS, side * COLS : (side + 1) * COLS],
                    rhs_sems.at[2 * n + side],
                )
            )
    chunks = [copies[8 + 4 * k : 12 + 4 * k] for k in range(4)]
    for copy in copies[:8] + chunks[0]:
        copy.start()
    for copy in copies[:8]:
        copy.wait()
    for k in range(4):
        for copy in chunks[k]:
            copy.wait()
        if k < 3:
            for copy in chunks[k + 1]:
                copy.start()
        at = slice(k * 2 * ROWS, (k + 1) * 2 * ROWS)
        term = dot(lhs[:, at], rhs[at, :], 1, 0)
        if k:
            acc[...] += term
        else:
            acc[...] = term
    own = rhs[rows_of(core, HALF), :].astype(jnp.float32)
    out = (math.sqrt(QD) * (linear_coef * own + acc[...])).astype(jnp.bfloat16)
    mine_ref[rows_of(core, HALF), :] = out[:, :COLS]
    other_ref[...] = out[:, COLS:]


def update_of(pieces, blocks, other_blocks):
    inside = pl.BlockSpec(memory_space=pltpu.VMEM)
    mine = jax.ShapeDtypeStruct((ROWS, COLS), jnp.bfloat16)
    other = jax.ShapeDtypeStruct((HALF, COLS), jnp.bfloat16)
    return pl.pallas_call(
        update_kernel,
        in_specs=[pl.BlockSpec(memory_space=pl.ANY)] * 24,
        out_specs=[inside, inside],
        out_shape=[mine, other],
        scratch_shapes=[
            pltpu.VMEM((HALF, D), jnp.bfloat16),
            pltpu.VMEM((D, 2 * COLS), jnp.bfloat16),
            pltpu.VMEM((HALF, 2 * COLS), jnp.float32),
            pltpu.SemaphoreType.DMA((8,)),
            pltpu.SemaphoreType.DMA((16,)),
        ],
        compiler_params=pltpu.CompilerParams(vmem_limit_bytes=VMEM),
        cost_estimate=cost(1, 1),
        name="update",
    )(*pieces, *blocks, *other_blocks)


def per_device(inputs, queries, key_rows, values, attn_out, grad_out, momentum, iterate):
    yh, _, _, yl, core = place()
    together = lax.optimization_barrier
    f32, bf16 = jnp.float32, jnp.bfloat16

    own = iterate
    below = move(own, X_UP)
    above = move(own, X_DOWN)
    across = move(own, Y_HI)
    kv_index = (lax.axis_index("grid") // 2).astype(jnp.int32).reshape(1)
    grad_query_t = attention(queries, key_rows, values, attn_out, grad_out, kv_index)
    below, above, across, grad_query_t = together((below, above, across, grad_query_t))

    far_top, far_bottom = move(below[:HALF], X_UP), move(above[HALF:], X_DOWN)
    own_other, above_other, below_other = move(own, CORE), move(above, CORE), move(below, CORE)
    far_partial = gradient_partial(grad_query_t, inputs, 1 - yh)
    far_top, far_bottom, above, across, grad_query_t, far_partial = together(
        (far_top, far_bottom, above, across, grad_query_t, far_partial)
    )
    own_other, above_other, below_other, far_top = together(
        (own_other, above_other, below_other, far_top)
    )
    far = jnp.concatenate([far_top, far_bottom])

    across_below = move(across, X_UP)
    across_above = move(across, X_DOWN)
    across_far = move(far, Y_HI)
    far_other, across_other = move(far, CORE), move(across, CORE)
    near, near1, near2, near3 = gram_partial(
        own,
        own_other,
        (own, above, far, below),
        (own_other, above_other, far_other, below_other),
    )
    far_partial, near = together((far_partial, near))
    far_terms = lax.all_to_all(far_partial, "x", 0, 0, tiled=True)
    near1, near3 = move(near1, Z_UP), move(near3, Z_DOWN)
    across_below, across_above, across_far, across_other, near, near1, near2, near3 = together(
        (across_below, across_above, across_far, across_other, near, near1, near2, near3)
    )

    far_swapped = move(across_far, CORE)
    above_swapped = move(across_above, CORE)
    below_swapped = move(across_below, CORE)
    near2 = move(near2, Z_FAR)
    far_swapped, above_swapped, below_swapped = together(
        (far_swapped, above_swapped, below_swapped)
    )
    other, other1, other2, other3 = gram_partial(
        own,
        own_other,
        (across, across_above, across_far, across_below),
        (across_other, above_swapped, far_swapped, below_swapped),
    )
    other, other1, other2, other3, near2 = together((other, other1, other2, other3, near2))
    other1, other2, other3 = move(other1, Z_UP), move(other2, Z_FAR), move(other3, Z_DOWN)
    near = near + near1.astype(f32) + near3.astype(f32) + near2.astype(f32)
    other1, other2, other3, near = together((other1, other2, other3, near))
    other = other + other1.astype(f32) + other3.astype(f32) + other2.astype(f32)
    same = yh == yl
    kept = jnp.where(same, near, other)
    rows = (kept + move(jnp.where(same, other, near).astype(bf16), Y_LO).astype(f32)).astype(bf16)

    rows, far_terms, grad_query_t = together((rows, far_terms, grad_query_t))

    def along_x(piece):
        return lax.all_to_all(jnp.broadcast_to(piece, (4, HALF, ROWS)), "x", 0, 0, tiled=True)

    lo, z_far = move(rows, Y_LO), move(rows, Z_FAR)
    across_rows = move(rows, Y_HI)
    here = along_x(rows)
    partial = gradient_partial(grad_query_t, inputs, yh)
    far_term = sum(far_terms[n].astype(f32) for n in range(4)).astype(bf16)
    rows, lo, z_far, across_rows, here, partial, far_term = together(
        (rows, lo, z_far, across_rows, here, partial, far_term)
    )
    z_below, z_above = move(rows, Z_UP), move(rows, Z_DOWN)
    lo_below, lo_above, lo_far = move(lo, Z_UP), move(lo, Z_DOWN), move(z_far, Y_LO)
    there = along_x(across_rows)
    partial, lo_below = together((partial, lo_below))
    terms = lax.all_to_all(partial, "x", 0, 0, tiled=True)
    z_below, z_above, lo_below, lo_above, lo_far, there, here, far_term = together(
        (z_below, z_above, lo_below, lo_above, lo_far, there, here, far_term)
    )
    combined = square(
        (rows, z_above, z_far, z_below, lo, lo_above, lo_far, lo_below),
        (here, there, move(here, CORE), move(there, CORE)),
    )

    z_below, z_above = move(combined, Z_UP), move(combined, Z_DOWN)
    lo, z_far = move(combined, Y_LO), move(combined, Z_FAR)
    far_term = move(far_term, Y_HI)
    z_below, z_above, lo, z_far, far_term = together((z_below, z_above, lo, z_far, far_term))
    lo_below, lo_above, lo_far = move(lo, Z_UP), move(lo, Z_DOWN), move(z_far, Y_LO)
    momentum_next = momentum_of(momentum, terms, far_term)
    lo_below, lo_above, lo_far, momentum_next = together(
        (lo_below, lo_above, lo_far, momentum_next)
    )
    mine, theirs = update_of(
        (combined, z_above, z_far, z_below, lo, lo_above, lo_far, lo_below),
        (own, above, far, below, across, across_above, across_far, across_below),
        (own_other, above_other, far_other, below_other, across_other)
        + (above_swapped, far_swapped, below_swapped),
    )
    update = lax.dynamic_update_slice(mine, move(theirs, CORE), ((1 - core) * HALF, 0))
    return (momentum_next, update)


def solution(mesh):
    parts = jax.sharding.Mesh(mesh.devices.reshape(2, 4, 16), ("y_hi", "x", "grid"))
    dp = ("y_hi", "x")
    rows, both = P(dp, None), P(dp, "grid")
    return jax.shard_map(
        per_device,
        mesh=parts,
        in_specs=(rows, both, rows, rows, both, both, both, both),
        out_specs=(both, both),
        check_vma=False,
    )
```

```python
import math

import jax
import jax.numpy as jnp
import numpy as np
from jax import lax
from jax.experimental import pallas as pl
from jax.experimental.pallas import tpu as pltpu
from jax.sharding import PartitionSpec as P

HEADS = 96
KV_HEADS = 8
HEAD_DIM = 128
SEQ_LEN = 1024
QD = 12288
D = 5120
ROWS = 640
COLS = 768
HALF = 320
QUART = 160
SHAPE = (2, 4, 4, 2, 2)

linear_coef = 3.4445
cubic_coef = -4.775
quintic_coef = 2.0315

VMEM = 60 * 1024 * 1024


def make_perm(move):
    pairs = []
    for source in range(128):
        place = np.unravel_index(source, SHAPE)
        target = [int(a) % b for a, b in zip(move(*place), SHAPE)]
        pairs.append((source, int(np.ravel_multi_index(target, SHAPE))))
    return pairs


X_UP = make_perm(lambda yh, x, z, yl, c: (yh, x + 1, z, yl, c))
X_DOWN = make_perm(lambda yh, x, z, yl, c: (yh, x - 1, z, yl, c))
Z_UP = make_perm(lambda yh, x, z, yl, c: (yh, x, z + 1, yl, c))
Z_DOWN = make_perm(lambda yh, x, z, yl, c: (yh, x, z - 1, yl, c))
Z_FAR = make_perm(lambda yh, x, z, yl, c: (yh, x, z + 2, yl, c))
X_FAR = make_perm(lambda yh, x, z, yl, c: (yh, x + 2, z, yl, c))
Y_HI = make_perm(lambda yh, x, z, yl, c: (yh + 1, x, z, yl, c))
Y_LO = make_perm(lambda yh, x, z, yl, c: (yh, x, z, yl + 1, c))
CORE = make_perm(lambda yh, x, z, yl, c: (yh, x, z, yl, c + 1))


def move(array, perm):
    return lax.ppermute(array, ("y_hi", "x", "grid"), perm)


def place():
    grid = lax.axis_index("grid")
    return (
        lax.axis_index("y_hi"),
        lax.axis_index("x"),
        grid // 4,
        (grid // 2) % 2,
        grid % 2,
    )


def cost(flops, bytes_accessed, transcendentals=0):
    return pl.CostEstimate(
        flops=flops, bytes_accessed=bytes_accessed, transcendentals=transcendentals
    )


def dot(a, b, ca, cb):
    return lax.dot_general(a, b, (((ca,), (cb,)), ((), ())), preferred_element_type=jnp.float32)


def attention_kernel(q_ref, k_ref, v_ref, o_ref, do_ref, out_ref):
    block = 256
    scale = 1.0 / math.sqrt(HEAD_DIM)
    rows = lax.broadcasted_iota(jnp.int32, (block, block), 0)
    cols = lax.broadcasted_iota(jnp.int32, (block, block), 1)
    keep = cols <= rows
    for r in range(SEQ_LEN // block):
        start, length = r * block, (r + 1) * block
        q = q_ref[start:length, :]
        do = do_ref[start:length, :]
        o = o_ref[start:length, :]
        delta = jnp.sum(do.astype(jnp.float32) * o.astype(jnp.float32), axis=-1, keepdims=True)
        diag = jnp.where(keep, dot(q, k_ref[start:length, :], 1, 1), -jnp.inf)
        row_max = jnp.max(diag, axis=-1, keepdims=True)
        if r:
            body = dot(q, k_ref[:start, :], 1, 1)
            row_max = jnp.maximum(row_max, jnp.max(body, axis=-1, keepdims=True))
        e = jnp.exp((diag - row_max) * scale)
        total = jnp.sum(e, axis=-1, keepdims=True)
        g = (e * (dot(do, v_ref[start:length, :], 1, 1) - delta)).astype(jnp.bfloat16)
        grad = dot(g, k_ref[start:length, :], 1, 0)
        if r:
            e = jnp.exp((body - row_max) * scale)
            total = total + jnp.sum(e, axis=-1, keepdims=True)
            g = (e * (dot(do, v_ref[:start, :], 1, 1) - delta)).astype(jnp.bfloat16)
            grad = grad + dot(g, k_ref[:start, :], 1, 0)
        grad = grad * (scale / total)
        out_ref[:, start:length] = grad.T.astype(jnp.bfloat16)


def attention(queries, keys, values, attn_out, grad_out, kv_index):
    heads = queries.shape[1] // HEAD_DIM
    mine = pl.BlockSpec((SEQ_LEN, HEAD_DIM), lambda h, kv: (0, h))
    shared = pl.BlockSpec((SEQ_LEN, HEAD_DIM), lambda h, kv: (0, kv[0]))

    def body(kv, *refs):
        attention_kernel(*refs)

    return pl.pallas_call(
        body,
        grid_spec=pltpu.PrefetchScalarGridSpec(
            num_scalar_prefetch=1,
            grid=(heads,),
            in_specs=[mine, shared, shared, mine, mine],
            out_specs=pl.BlockSpec((HEAD_DIM, SEQ_LEN), lambda h, kv: (h, 0)),
        ),
        out_shape=jax.ShapeDtypeStruct((heads * HEAD_DIM, SEQ_LEN), jnp.bfloat16),
        compiler_params=pltpu.CompilerParams(vmem_limit_bytes=VMEM),
        cost_estimate=cost(24 * 10**9, 8 * 10**6, 4 * 10**6),
        name="attention",
    )(kv_index, queries, keys, values, attn_out, grad_out)


def gradient_kernel(block_ref, gq_ref, in_ref, out_ref):
    out_ref[0] = dot(gq_ref[...], in_ref[...], 1, 0).astype(jnp.bfloat16)


def gradient_partial(grad_query_t, inputs, yh):
    return pl.pallas_call(
        gradient_kernel,
        grid_spec=pltpu.PrefetchScalarGridSpec(
            num_scalar_prefetch=1,
            grid=(4,),
            in_specs=[
                pl.BlockSpec((COLS, SEQ_LEN), lambda k, yh: (0, 0)),
                pl.BlockSpec((SEQ_LEN, ROWS), lambda k, yh: (0, yh[0] * 4 + k)),
            ],
            out_specs=pl.BlockSpec((1, COLS, ROWS), lambda k, yh: (k, 0, 0)),
        ),
        out_shape=jax.ShapeDtypeStruct((4, COLS, ROWS), jnp.bfloat16),
        compiler_params=pltpu.CompilerParams(vmem_limit_bytes=VMEM),
        cost_estimate=cost(16 * ROWS * COLS * SEQ_LEN, 12 * 10**6),
        name="gradient",
    )(yh.astype(jnp.int32).reshape(1), grad_query_t, inputs)


def momentum_kernel(m_ref, g_ref, h_ref, out_ref):
    total = h_ref[...].astype(jnp.float32)
    for n in range(4):
        total = total + g_ref[n].astype(jnp.float32)
    out_ref[...] = 0.95 * m_ref[...] + total.T


def momentum_of(momentum, terms, term):
    mine = pl.BlockSpec((128, COLS), lambda k: (k, 0))
    return pl.pallas_call(
        momentum_kernel,
        grid=(ROWS // 128,),
        in_specs=[
            mine,
            pl.BlockSpec((4, COLS, 128), lambda k: (0, 0, k)),
            pl.BlockSpec((COLS, 128), lambda k: (0, k)),
        ],
        out_specs=mine,
        out_shape=jax.ShapeDtypeStruct((ROWS, COLS), jnp.float32),
        compiler_params=pltpu.CompilerParams(vmem_limit_bytes=VMEM),
        cost_estimate=cost(9 * ROWS * COLS, 9 * 10**6),
        name="momentum",
    )(momentum, terms, term)


def gram_kernel(*refs):
    own, own_other = refs[8:10]
    outs, (lhs, rhs, acc, sems) = refs[10:14], refs[14:]
    _, x, z, _, core = place()
    copies = ([], [])
    for n, block in enumerate((own, own_other)):
        source = block.at[rows_of(core, HALF), :]
        copies[n].append(
            pltpu.make_async_copy(source, lhs.at[:, n * COLS : (n + 1) * COLS], sems.at[8 + n])
        )
    for n, block in enumerate(refs[:8]):
        slot = (x + n % 4 - z + 4) % 4
        side = slice(n // 4 * COLS, (n // 4 + 1) * COLS)
        copies[n // 4].append(
            pltpu.make_async_copy(block, rhs.at[rows_of(slot, ROWS), side], sems.at[n])
        )
    for copy in copies[0]:
        copy.start()
    for copy in copies[0]:
        copy.wait()
    for copy in copies[1]:
        copy.start()
    pairs = [slice(pair * 2 * ROWS, (pair + 1) * 2 * ROWS) for pair in range(2)]
    for at in pairs:
        acc[:, at] = dot(lhs[:, :COLS], rhs[at, :COLS], 1, 1)
    for copy in copies[1]:
        copy.wait()
    for pair, at in enumerate(pairs):
        value = acc[:, at] + dot(lhs[:, COLS:], rhs[at, COLS:], 1, 1)
        for n in range(2):
            out_ref = outs[pair * 2 + n]
            out_ref[...] = value[:, n * ROWS : (n + 1) * ROWS].astype(out_ref.dtype)


def gram_partial(own, own_other, blocks, other_blocks):
    shape = (HALF, ROWS)
    return pl.pallas_call(
        gram_kernel,
        in_specs=[pl.BlockSpec(memory_space=pl.ANY)] * 10,
        out_specs=[pl.BlockSpec(memory_space=pltpu.VMEM)] * 4,
        out_shape=[jax.ShapeDtypeStruct(shape, jnp.float32)]
        + [jax.ShapeDtypeStruct(shape, jnp.bfloat16)] * 3,
        scratch_shapes=[
            pltpu.VMEM((HALF, 2 * COLS), jnp.bfloat16),
            pltpu.VMEM((4 * ROWS, 2 * COLS), jnp.bfloat16),
            pltpu.VMEM((HALF, 4 * ROWS), jnp.float32),
            pltpu.SemaphoreType.DMA((10,)),
        ],
        compiler_params=pltpu.CompilerParams(vmem_limit_bytes=VMEM),
        cost_estimate=cost(1, 1),
        name="gram",
    )(*blocks, *other_blocks, own, own_other)


def piece_place(n):
    yh, x, z, yl, _ = place()
    return ((yl + n // 4 + yh) % 2) * 4 + (z + n % 4 - x + 4) % 4


def dp_block(n):
    yh, x, _, _, _ = place()
    return ((yh + n // 4) % 2) * 4 + (x + n % 4) % 4


def rows_of(index, size):
    return pl.ds(pl.multiple_of(index * size, size), size)


def square_kernel(*refs):
    grid_refs, dp_refs = refs[:8], refs[8:12]
    out_ref, lhs, rhs, acc, lhs_sems, rhs_sems = refs[12:]
    yh, _, z, yl, core = place()
    places = [((yl + n // 4 + yh) % 2) * 4 + (z + n % 4) % 4 for n in range(8)]
    copies = []
    for n, piece in enumerate(grid_refs):
        copies.append(
            pltpu.make_async_copy(piece, lhs.at[:, rows_of(places[n], ROWS)], lhs_sems.at[n])
        )
    for n in range(16):
        side = core if n < 8 else 1 - core
        copies.append(
            pltpu.make_async_copy(
                dp_refs[n // 4].at[n % 4],
                rhs.at[rows_of(n % 8 * 2 + side, HALF), :],
                rhs_sems.at[n],
            )
        )
    chunks = [[copies[8 + n] for n in (2 * k, 2 * k + 1, 2 * k + 8, 2 * k + 9)] for k in range(4)]
    for copy in copies[:8] + chunks[0]:
        copy.start()
    for copy in copies[:8]:
        copy.wait()
    for k in range(4):
        for copy in chunks[k]:
            copy.wait()
        if k < 3:
            for copy in chunks[k + 1]:
                copy.start()
        at = slice(k * 2 * ROWS, (k + 1) * 2 * ROWS)
        term = dot(lhs[:, at], rhs[at, :], 1, 0)
        if k:
            acc[...] += term
        else:
            acc[...] = term
    out = cubic_coef * lhs[:, rows_of(places[0], ROWS)].astype(jnp.float32)
    out_ref[...] = (out + quintic_coef * acc[...]).astype(jnp.bfloat16)


def square(over_grid, over_dp):
    return pl.pallas_call(
        square_kernel,
        in_specs=[pl.BlockSpec(memory_space=pl.ANY)] * 12,
        out_specs=pl.BlockSpec(memory_space=pltpu.VMEM),
        out_shape=jax.ShapeDtypeStruct((HALF, ROWS), jnp.bfloat16),
        scratch_shapes=[
            pltpu.VMEM((HALF, D), jnp.bfloat16),
            pltpu.VMEM((D, ROWS), jnp.bfloat16),
            pltpu.VMEM((HALF, ROWS), jnp.float32),
            pltpu.SemaphoreType.DMA((8,)),
            pltpu.SemaphoreType.DMA((16,)),
        ],
        compiler_params=pltpu.CompilerParams(vmem_limit_bytes=VMEM),
        cost_estimate=cost(4 * HALF * D * ROWS, 11 * 10**6),
        name="square",
    )(*over_grid, *over_dp)


def update_kernel(*refs):
    n_refs, x_refs = refs[:8], refs[8:24]
    mine_ref, other_ref, lhs, rhs, acc, lhs_sems, rhs_sems = refs[24:]
    core = place()[4]
    copies = []
    for n, piece in enumerate(n_refs):
        copies.append(
            pltpu.make_async_copy(piece, lhs.at[:, rows_of(piece_place(n), ROWS)], lhs_sems.at[n])
        )
    for n in range(8):
        for side in range(2):
            copies.append(
                pltpu.make_async_copy(
                    x_refs[side * 8 + n],
                    rhs.at[n * ROWS : (n + 1) * ROWS, side * COLS : (side + 1) * COLS],
                    rhs_sems.at[2 * n + side],
                )
            )
    chunks = [copies[8 + 4 * k : 12 + 4 * k] for k in range(4)]
    for copy in copies[:8] + chunks[0]:
        copy.start()
    for copy in copies[:8]:
        copy.wait()
    for k in range(4):
        for copy in chunks[k]:
            copy.wait()
        if k < 3:
            for copy in chunks[k + 1]:
                copy.start()
        at = slice(k * 2 * ROWS, (k + 1) * 2 * ROWS)
        term = dot(lhs[:, at], rhs[at, :], 1, 0)
        if k:
            acc[...] += term
        else:
            acc[...] = term
    own = rhs[rows_of(core, HALF), :].astype(jnp.float32)
    out = (math.sqrt(QD) * (linear_coef * own + acc[...])).astype(jnp.bfloat16)
    mine_ref[rows_of(core, HALF), :] = out[:, :COLS]
    other_ref[...] = out[:, COLS:]


def update_of(pieces, blocks, other_blocks):
    inside = pl.BlockSpec(memory_space=pltpu.VMEM)
    mine = jax.ShapeDtypeStruct((ROWS, COLS), jnp.bfloat16)
    other = jax.ShapeDtypeStruct((HALF, COLS), jnp.bfloat16)
    return pl.pallas_call(
        update_kernel,
        in_specs=[pl.BlockSpec(memory_space=pl.ANY)] * 24,
        out_specs=[inside, inside],
        out_shape=[mine, other],
        scratch_shapes=[
            pltpu.VMEM((HALF, D), jnp.bfloat16),
            pltpu.VMEM((D, 2 * COLS), jnp.bfloat16),
            pltpu.VMEM((HALF, 2 * COLS), jnp.float32),
            pltpu.SemaphoreType.DMA((8,)),
            pltpu.SemaphoreType.DMA((16,)),
        ],
        compiler_params=pltpu.CompilerParams(vmem_limit_bytes=VMEM),
        cost_estimate=cost(1, 1),
        name="update",
    )(*pieces, *blocks, *other_blocks)


def per_device(inputs, queries, key_rows, values, attn_out, grad_out, momentum, iterate):
    yh, _, _, yl, core = place()
    together = lax.optimization_barrier
    f32, bf16 = jnp.float32, jnp.bfloat16

    own = iterate
    across = move(own, Y_HI)
    above = move(own, X_DOWN)
    below = move(own, X_UP)
    kv_index = (lax.axis_index("grid") // 2).astype(jnp.int32).reshape(1)
    grad_query_t = attention(queries, key_rows, values, attn_out, grad_out, kv_index)
    across, above, below, grad_query_t = together((across, above, below, grad_query_t))

    far_top, far_bottom = move(below[:HALF], X_UP), move(above[HALF:], X_DOWN)
    own_other, above_other, below_other = move(own, CORE), move(above, CORE), move(below, CORE)
    far_partial = gradient_partial(grad_query_t, inputs, 1 - yh)
    far_top, far_bottom, above, across, grad_query_t, far_partial = together(
        (far_top, far_bottom, above, across, grad_query_t, far_partial)
    )
    own_other, above_other, below_other, far_top = together(
        (own_other, above_other, below_other, far_top)
    )
    far = jnp.concatenate([far_top, far_bottom])

    across_below = move(across, X_UP)
    across_above = move(across, X_DOWN)
    across_far = move(far, Y_HI)
    far_other, across_other = move(far, CORE), move(across, CORE)
    near, near1, near2, near3 = gram_partial(
        own,
        own_other,
        (own, above, far, below),
        (own_other, above_other, far_other, below_other),
    )
    far_partial, near = together((far_partial, near))
    far_terms = lax.all_to_all(far_partial, "x", 0, 0, tiled=True)
    near1, near3 = move(near1, Z_UP), move(near3, Z_DOWN)
    across_below, across_above, across_far, across_other, near, near1, near2, near3 = together(
        (across_below, across_above, across_far, across_other, near, near1, near2, near3)
    )

    far_swapped = move(across_far, CORE)
    above_swapped = move(across_above, CORE)
    below_swapped = move(across_below, CORE)
    near2 = move(near2, Z_FAR)
    far_swapped, above_swapped, below_swapped = together(
        (far_swapped, above_swapped, below_swapped)
    )
    other, other1, other2, other3 = gram_partial(
        own,
        own_other,
        (across, across_above, across_far, across_below),
        (across_other, above_swapped, far_swapped, below_swapped),
    )
    other, other1, other2, other3, near2 = together((other, other1, other2, other3, near2))
    other1, other2, other3 = move(other1, Z_UP), move(other2, Z_FAR), move(other3, Z_DOWN)
    near = near + near1.astype(f32) + near3.astype(f32) + near2.astype(f32)
    other1, other2, other3, near = together((other1, other2, other3, near))
    other = other + other1.astype(f32) + other3.astype(f32) + other2.astype(f32)
    same = yh == yl
    kept = jnp.where(same, near, other)
    rows = (kept + move(jnp.where(same, other, near).astype(bf16), Y_LO).astype(f32)).astype(bf16)

    rows, far_terms, grad_query_t = together((rows, far_terms, grad_query_t))

    def along_x(piece):
        return lax.all_to_all(jnp.broadcast_to(piece, (4, HALF, ROWS)), "x", 0, 0, tiled=True)

    lo, z_far = move(rows, Y_LO), move(rows, Z_FAR)
    across_rows = move(rows, Y_HI)
    here = along_x(rows)
    partial = gradient_partial(grad_query_t, inputs, yh)
    far_term = sum(far_terms[n].astype(f32) for n in range(4)).astype(bf16)
    rows, lo, z_far, across_rows, here, partial, far_term = together(
        (rows, lo, z_far, across_rows, here, partial, far_term)
    )
    z_below, z_above = move(rows, Z_UP), move(rows, Z_DOWN)
    lo_below, lo_above, lo_far = move(lo, Z_UP), move(lo, Z_DOWN), move(z_far, Y_LO)
    there = along_x(across_rows)
    partial, lo_below = together((partial, lo_below))
    terms = lax.all_to_all(partial, "x", 0, 0, tiled=True)
    z_below, z_above, lo_below, lo_above, lo_far, there, here, far_term = together(
        (z_below, z_above, lo_below, lo_above, lo_far, there, here, far_term)
    )
    combined = square(
        (rows, z_above, z_far, z_below, lo, lo_above, lo_far, lo_below),
        (here, there, move(here, CORE), move(there, CORE)),
    )

    z_far, lo = move(combined, Z_FAR), move(combined, Y_LO)
    z_above, z_below = move(combined, Z_DOWN), move(combined, Z_UP)
    far_term = move(far_term, Y_HI)
    z_far, lo, z_above, z_below, far_term = together((z_far, lo, z_above, z_below, far_term))
    lo_below, lo_above, lo_far = move(lo, Z_UP), move(lo, Z_DOWN), move(z_far, Y_LO)
    momentum_next = momentum_of(momentum, terms, far_term)
    lo_below, lo_above, lo_far, momentum_next = together(
        (lo_below, lo_above, lo_far, momentum_next)
    )
    mine, theirs = update_of(
        (combined, z_above, z_far, z_below, lo, lo_above, lo_far, lo_below),
        (own, above, far, below, across, across_above, across_far, across_below),
        (own_other, above_other, far_other, below_other, across_other)
        + (above_swapped, far_swapped, below_swapped),
    )
    update = lax.dynamic_update_slice(mine, move(theirs, CORE), ((1 - core) * HALF, 0))
    return (momentum_next, update)


def solution(mesh):
    parts = jax.sharding.Mesh(mesh.devices.reshape(2, 4, 16), ("y_hi", "x", "grid"))
    dp = ("y_hi", "x")
    rows, both = P(dp, None), P(dp, "grid")
    return jax.shard_map(
        per_device,
        mesh=parts,
        in_specs=(rows, both, rows, rows, both, both, both, both),
        out_specs=(both, both),
        check_vma=False,
    )
```

```python
import math

import jax
import jax.numpy as jnp
import numpy as np
from jax import lax
from jax.experimental import pallas as pl
from jax.experimental.pallas import tpu as pltpu
from jax.sharding import PartitionSpec as P

HEADS = 96
KV_HEADS = 8
HEAD_DIM = 128
SEQ_LEN = 1024
QD = 12288
D = 5120
ROWS = 640
COLS = 768
HALF = 320
QUART = 160
SHAPE = (2, 4, 4, 2, 2)

linear_coef = 3.4445
cubic_coef = -4.775
quintic_coef = 2.0315

VMEM = 60 * 1024 * 1024


def make_perm(move):
    pairs = []
    for source in range(128):
        place = np.unravel_index(source, SHAPE)
        target = [int(a) % b for a, b in zip(move(*place), SHAPE)]
        pairs.append((source, int(np.ravel_multi_index(target, SHAPE))))
    return pairs


X_UP = make_perm(lambda yh, x, z, yl, c: (yh, x + 1, z, yl, c))
X_DOWN = make_perm(lambda yh, x, z, yl, c: (yh, x - 1, z, yl, c))
Z_UP = make_perm(lambda yh, x, z, yl, c: (yh, x, z + 1, yl, c))
Z_DOWN = make_perm(lambda yh, x, z, yl, c: (yh, x, z - 1, yl, c))
Z_FAR = make_perm(lambda yh, x, z, yl, c: (yh, x, z + 2, yl, c))
X_FAR = make_perm(lambda yh, x, z, yl, c: (yh, x + 2, z, yl, c))
Y_HI = make_perm(lambda yh, x, z, yl, c: (yh + 1, x, z, yl, c))
Y_LO = make_perm(lambda yh, x, z, yl, c: (yh, x, z, yl + 1, c))
CORE = make_perm(lambda yh, x, z, yl, c: (yh, x, z, yl, c + 1))


def move(array, perm):
    return lax.ppermute(array, ("y_hi", "x", "grid"), perm)


def place():
    grid = lax.axis_index("grid")
    return (
        lax.axis_index("y_hi"),
        lax.axis_index("x"),
        grid // 4,
        (grid // 2) % 2,
        grid % 2,
    )


def cost(flops, bytes_accessed, transcendentals=0):
    return pl.CostEstimate(
        flops=flops, bytes_accessed=bytes_accessed, transcendentals=transcendentals
    )


def dot(a, b, ca, cb):
    return lax.dot_general(a, b, (((ca,), (cb,)), ((), ())), preferred_element_type=jnp.float32)


def attention_kernel(q_ref, k_ref, v_ref, o_ref, do_ref, out_ref):
    block = 256
    scale = 1.0 / math.sqrt(HEAD_DIM)
    rows = lax.broadcasted_iota(jnp.int32, (block, block), 0)
    cols = lax.broadcasted_iota(jnp.int32, (block, block), 1)
    keep = cols <= rows
    for r in range(SEQ_LEN // block):
        start, length = r * block, (r + 1) * block
        q = q_ref[start:length, :]
        do = do_ref[start:length, :]
        o = o_ref[start:length, :]
        delta = jnp.sum(do.astype(jnp.float32) * o.astype(jnp.float32), axis=-1, keepdims=True)
        diag = jnp.where(keep, dot(q, k_ref[start:length, :], 1, 1), -jnp.inf)
        row_max = jnp.max(diag, axis=-1, keepdims=True)
        if r:
            body = dot(q, k_ref[:start, :], 1, 1)
            row_max = jnp.maximum(row_max, jnp.max(body, axis=-1, keepdims=True))
        e = jnp.exp((diag - row_max) * scale)
        total = jnp.sum(e, axis=-1, keepdims=True)
        g = (e * (dot(do, v_ref[start:length, :], 1, 1) - delta)).astype(jnp.bfloat16)
        grad = dot(g, k_ref[start:length, :], 1, 0)
        if r:
            e = jnp.exp((body - row_max) * scale)
            total = total + jnp.sum(e, axis=-1, keepdims=True)
            g = (e * (dot(do, v_ref[:start, :], 1, 1) - delta)).astype(jnp.bfloat16)
            grad = grad + dot(g, k_ref[:start, :], 1, 0)
        grad = grad * (scale / total)
        out_ref[:, start:length] = grad.T.astype(jnp.bfloat16)


def attention(queries, keys, values, attn_out, grad_out, kv_index):
    heads = queries.shape[1] // HEAD_DIM
    mine = pl.BlockSpec((SEQ_LEN, HEAD_DIM), lambda h, kv: (0, h))
    shared = pl.BlockSpec((SEQ_LEN, HEAD_DIM), lambda h, kv: (0, kv[0]))

    def body(kv, *refs):
        attention_kernel(*refs)

    return pl.pallas_call(
        body,
        grid_spec=pltpu.PrefetchScalarGridSpec(
            num_scalar_prefetch=1,
            grid=(heads,),
            in_specs=[mine, shared, shared, mine, mine],
            out_specs=pl.BlockSpec((HEAD_DIM, SEQ_LEN), lambda h, kv: (h, 0)),
        ),
        out_shape=jax.ShapeDtypeStruct((heads * HEAD_DIM, SEQ_LEN), jnp.bfloat16),
        compiler_params=pltpu.CompilerParams(vmem_limit_bytes=VMEM),
        cost_estimate=cost(24 * 10**9, 8 * 10**6, 4 * 10**6),
        name="attention",
    )(kv_index, queries, keys, values, attn_out, grad_out)


def gradient_kernel(block_ref, gq_ref, in_ref, out_ref):
    out_ref[0] = dot(gq_ref[...], in_ref[...], 1, 0).astype(jnp.bfloat16)


def gradient_partial(grad_query_t, inputs, yh):
    return pl.pallas_call(
        gradient_kernel,
        grid_spec=pltpu.PrefetchScalarGridSpec(
            num_scalar_prefetch=1,
            grid=(4,),
            in_specs=[
                pl.BlockSpec((COLS, SEQ_LEN), lambda k, yh: (0, 0)),
                pl.BlockSpec((SEQ_LEN, ROWS), lambda k, yh: (0, yh[0] * 4 + k)),
            ],
            out_specs=pl.BlockSpec((1, COLS, ROWS), lambda k, yh: (k, 0, 0)),
        ),
        out_shape=jax.ShapeDtypeStruct((4, COLS, ROWS), jnp.bfloat16),
        compiler_params=pltpu.CompilerParams(vmem_limit_bytes=VMEM),
        cost_estimate=cost(16 * ROWS * COLS * SEQ_LEN, 12 * 10**6),
        name="gradient",
    )(yh.astype(jnp.int32).reshape(1), grad_query_t, inputs)


def momentum_kernel(m_ref, g_ref, h_ref, out_ref):
    total = h_ref[...].astype(jnp.float32)
    for n in range(4):
        total = total + g_ref[n].astype(jnp.float32)
    out_ref[...] = 0.95 * m_ref[...] + total.T


def momentum_of(momentum, terms, term):
    mine = pl.BlockSpec((128, COLS), lambda k: (k, 0))
    return pl.pallas_call(
        momentum_kernel,
        grid=(ROWS // 128,),
        in_specs=[
            mine,
            pl.BlockSpec((4, COLS, 128), lambda k: (0, 0, k)),
            pl.BlockSpec((COLS, 128), lambda k: (0, k)),
        ],
        out_specs=mine,
        out_shape=jax.ShapeDtypeStruct((ROWS, COLS), jnp.float32),
        compiler_params=pltpu.CompilerParams(vmem_limit_bytes=VMEM),
        cost_estimate=cost(9 * ROWS * COLS, 9 * 10**6),
        name="momentum",
    )(momentum, terms, term)


def gram_kernel(*refs):
    own, own_other = refs[8:10]
    outs, (lhs, rhs, acc, sems) = refs[10:14], refs[14:]
    _, x, z, _, core = place()
    copies = ([], [])
    for n, block in enumerate((own, own_other)):
        source = block.at[rows_of(core, HALF), :]
        copies[n].append(
            pltpu.make_async_copy(source, lhs.at[:, n * COLS : (n + 1) * COLS], sems.at[8 + n])
        )
    for n, block in enumerate(refs[:8]):
        slot = (x + n % 4 - z + 4) % 4
        side = slice(n // 4 * COLS, (n // 4 + 1) * COLS)
        copies[n // 4].append(
            pltpu.make_async_copy(block, rhs.at[rows_of(slot, ROWS), side], sems.at[n])
        )
    for copy in copies[0]:
        copy.start()
    for copy in copies[0]:
        copy.wait()
    for copy in copies[1]:
        copy.start()
    pairs = [slice(pair * 2 * ROWS, (pair + 1) * 2 * ROWS) for pair in range(2)]
    for at in pairs:
        acc[:, at] = dot(lhs[:, :COLS], rhs[at, :COLS], 1, 1)
    for copy in copies[1]:
        copy.wait()
    for pair, at in enumerate(pairs):
        value = acc[:, at] + dot(lhs[:, COLS:], rhs[at, COLS:], 1, 1)
        for n in range(2):
            out_ref = outs[pair * 2 + n]
            out_ref[...] = value[:, n * ROWS : (n + 1) * ROWS].astype(out_ref.dtype)


def gram_partial(own, own_other, blocks, other_blocks):
    shape = (HALF, ROWS)
    return pl.pallas_call(
        gram_kernel,
        in_specs=[pl.BlockSpec(memory_space=pl.ANY)] * 10,
        out_specs=[pl.BlockSpec(memory_space=pltpu.VMEM)] * 4,
        out_shape=[jax.ShapeDtypeStruct(shape, jnp.float32)]
        + [jax.ShapeDtypeStruct(shape, jnp.bfloat16)] * 3,
        scratch_shapes=[
            pltpu.VMEM((HALF, 2 * COLS), jnp.bfloat16),
            pltpu.VMEM((4 * ROWS, 2 * COLS), jnp.bfloat16),
            pltpu.VMEM((HALF, 4 * ROWS), jnp.float32),
            pltpu.SemaphoreType.DMA((10,)),
        ],
        compiler_params=pltpu.CompilerParams(vmem_limit_bytes=VMEM),
        cost_estimate=cost(1, 1),
        name="gram",
    )(*blocks, *other_blocks, own, own_other)


def piece_place(n):
    yh, x, z, yl, _ = place()
    return ((yl + n // 4 + yh) % 2) * 4 + (z + n % 4 - x + 4) % 4


def dp_block(n):
    yh, x, _, _, _ = place()
    return ((yh + n // 4) % 2) * 4 + (x + n % 4) % 4


def rows_of(index, size):
    return pl.ds(pl.multiple_of(index * size, size), size)


def square_kernel(*refs):
    grid_refs, dp_refs = refs[:8], refs[8:12]
    out_ref, lhs, rhs, acc, lhs_sems, rhs_sems = refs[12:]
    yh, _, z, yl, core = place()
    places = [((yl + n // 4 + yh) % 2) * 4 + (z + n % 4) % 4 for n in range(8)]
    copies = []
    for n, piece in enumerate(grid_refs):
        copies.append(
            pltpu.make_async_copy(piece, lhs.at[:, rows_of(places[n], ROWS)], lhs_sems.at[n])
        )
    for n in range(16):
        side = core if n < 8 else 1 - core
        copies.append(
            pltpu.make_async_copy(
                dp_refs[n // 4].at[n % 4],
                rhs.at[rows_of(n % 8 * 2 + side, HALF), :],
                rhs_sems.at[n],
            )
        )
    chunks = [[copies[8 + n] for n in (2 * k, 2 * k + 1, 2 * k + 8, 2 * k + 9)] for k in range(4)]
    for copy in copies[:8] + chunks[0]:
        copy.start()
    for copy in copies[:8]:
        copy.wait()
    for k in range(4):
        for copy in chunks[k]:
            copy.wait()
        if k < 3:
            for copy in chunks[k + 1]:
                copy.start()
        at = slice(k * 2 * ROWS, (k + 1) * 2 * ROWS)
        term = dot(lhs[:, at], rhs[at, :], 1, 0)
        if k:
            acc[...] += term
        else:
            acc[...] = term
    out = cubic_coef * lhs[:, rows_of(places[0], ROWS)].astype(jnp.float32)
    out_ref[...] = (out + quintic_coef * acc[...]).astype(jnp.bfloat16)


def square(over_grid, over_dp):
    return pl.pallas_call(
        square_kernel,
        in_specs=[pl.BlockSpec(memory_space=pl.ANY)] * 12,
        out_specs=pl.BlockSpec(memory_space=pltpu.VMEM),
        out_shape=jax.ShapeDtypeStruct((HALF, ROWS), jnp.bfloat16),
        scratch_shapes=[
            pltpu.VMEM((HALF, D), jnp.bfloat16),
            pltpu.VMEM((D, ROWS), jnp.bfloat16),
            pltpu.VMEM((HALF, ROWS), jnp.float32),
            pltpu.SemaphoreType.DMA((8,)),
            pltpu.SemaphoreType.DMA((16,)),
        ],
        compiler_params=pltpu.CompilerParams(vmem_limit_bytes=VMEM),
        cost_estimate=cost(4 * HALF * D * ROWS, 11 * 10**6),
        name="square",
    )(*over_grid, *over_dp)


def update_kernel(*refs):
    n_refs, x_refs = refs[:8], refs[8:24]
    mine_ref, other_ref, lhs, rhs, acc, lhs_sems, rhs_sems = refs[24:]
    core = place()[4]
    copies = []
    for n, piece in enumerate(n_refs):
        copies.append(
            pltpu.make_async_copy(piece, lhs.at[:, rows_of(piece_place(n), ROWS)], lhs_sems.at[n])
        )
    for n in range(8):
        for side in range(2):
            copies.append(
                pltpu.make_async_copy(
                    x_refs[side * 8 + n],
                    rhs.at[n * ROWS : (n + 1) * ROWS, side * COLS : (side + 1) * COLS],
                    rhs_sems.at[2 * n + side],
                )
            )
    chunks = [copies[8 + 4 * k : 12 + 4 * k] for k in range(4)]
    for copy in copies[:8] + chunks[0]:
        copy.start()
    for copy in copies[:8]:
        copy.wait()
    for k in range(4):
        for copy in chunks[k]:
            copy.wait()
        if k < 3:
            for copy in chunks[k + 1]:
                copy.start()
        at = slice(k * 2 * ROWS, (k + 1) * 2 * ROWS)
        term = dot(lhs[:, at], rhs[at, :], 1, 0)
        if k:
            acc[...] += term
        else:
            acc[...] = term
    own = rhs[rows_of(core, HALF), :].astype(jnp.float32)
    out = (math.sqrt(QD) * (linear_coef * own + acc[...])).astype(jnp.bfloat16)
    mine_ref[rows_of(core, HALF), :] = out[:, :COLS]
    other_ref[...] = out[:, COLS:]


def update_of(pieces, blocks, other_blocks):
    inside = pl.BlockSpec(memory_space=pltpu.VMEM)
    mine = jax.ShapeDtypeStruct((ROWS, COLS), jnp.bfloat16)
    other = jax.ShapeDtypeStruct((HALF, COLS), jnp.bfloat16)
    return pl.pallas_call(
        update_kernel,
        in_specs=[pl.BlockSpec(memory_space=pl.ANY)] * 24,
        out_specs=[inside, inside],
        out_shape=[mine, other],
        scratch_shapes=[
            pltpu.VMEM((HALF, D), jnp.bfloat16),
            pltpu.VMEM((D, 2 * COLS), jnp.bfloat16),
            pltpu.VMEM((HALF, 2 * COLS), jnp.float32),
            pltpu.SemaphoreType.DMA((8,)),
            pltpu.SemaphoreType.DMA((16,)),
        ],
        compiler_params=pltpu.CompilerParams(vmem_limit_bytes=VMEM),
        cost_estimate=cost(1, 1),
        name="update",
    )(*pieces, *blocks, *other_blocks)


def per_device(inputs, queries, key_rows, values, attn_out, grad_out, momentum, iterate):
    yh, _, _, yl, core = place()
    together = lax.optimization_barrier
    f32, bf16 = jnp.float32, jnp.bfloat16

    own = iterate
    across = move(own, Y_HI)
    above = move(own, X_DOWN)
    below = move(own, X_UP)
    kv_index = (lax.axis_index("grid") // 2).astype(jnp.int32).reshape(1)
    grad_query_t = attention(queries, key_rows, values, attn_out, grad_out, kv_index)
    across, above, below, grad_query_t = together((across, above, below, grad_query_t))

    far_top, far_bottom = move(below[:HALF], X_UP), move(above[HALF:], X_DOWN)
    own_other, above_other, below_other = move(own, CORE), move(above, CORE), move(below, CORE)
    far_partial = gradient_partial(grad_query_t, inputs, 1 - yh)
    far_top, far_bottom, above, across, grad_query_t, far_partial = together(
        (far_top, far_bottom, above, across, grad_query_t, far_partial)
    )
    own_other, above_other, below_other, far_top = together(
        (own_other, above_other, below_other, far_top)
    )
    far = jnp.concatenate([far_top, far_bottom])

    across_below = move(across, X_UP)
    across_above = move(across, X_DOWN)
    across_far = move(far, Y_HI)
    far_other, across_other = move(far, CORE), move(across, CORE)
    near, near1, near2, near3 = gram_partial(
        own,
        own_other,
        (own, above, far, below),
        (own_other, above_other, far_other, below_other),
    )
    far_partial, near = together((far_partial, near))
    far_terms = lax.all_to_all(far_partial, "x", 0, 0, tiled=True)
    near1, near3 = move(near1, Z_UP), move(near3, Z_DOWN)
    across_below, across_above, across_far, across_other, near, near1, near2, near3 = together(
        (across_below, across_above, across_far, across_other, near, near1, near2, near3)
    )

    far_swapped = move(across_far, CORE)
    above_swapped = move(across_above, CORE)
    below_swapped = move(across_below, CORE)
    near2 = move(near2, Z_FAR)
    far_swapped, above_swapped, below_swapped = together(
        (far_swapped, above_swapped, below_swapped)
    )
    other, other1, other2, other3 = gram_partial(
        own,
        own_other,
        (across, across_above, across_far, across_below),
        (across_other, above_swapped, far_swapped, below_swapped),
    )
    other, other1, other2, other3, near2 = together((other, other1, other2, other3, near2))
    other1, other2, other3 = move(other1, Z_UP), move(other2, Z_FAR), move(other3, Z_DOWN)
    near = near + near1.astype(f32) + near3.astype(f32) + near2.astype(f32)
    other2, other3, other1, near = together((other2, other3, other1, near))
    other = other + other1.astype(f32) + other3.astype(f32) + other2.astype(f32)
    same = yh == yl
    kept = jnp.where(same, near, other)
    rows = (kept + move(jnp.where(same, other, near).astype(bf16), Y_LO).astype(f32)).astype(bf16)

    rows, far_terms, grad_query_t = together((rows, far_terms, grad_query_t))

    def along_x(piece):
        return lax.all_to_all(jnp.broadcast_to(piece, (4, HALF, ROWS)), "x", 0, 0, tiled=True)

    lo, z_far = move(rows, Y_LO), move(rows, Z_FAR)
    across_rows = move(rows, Y_HI)
    here = along_x(rows)
    partial = gradient_partial(grad_query_t, inputs, yh)
    far_term = sum(far_terms[n].astype(f32) for n in range(4)).astype(bf16)
    rows, lo, z_far, across_rows, here, partial, far_term = together(
        (rows, lo, z_far, across_rows, here, partial, far_term)
    )
    z_below, z_above = move(rows, Z_UP), move(rows, Z_DOWN)
    lo_below, lo_above, lo_far = move(lo, Z_UP), move(lo, Z_DOWN), move(z_far, Y_LO)
    there = along_x(across_rows)
    partial, lo_below = together((partial, lo_below))
    terms = lax.all_to_all(partial, "x", 0, 0, tiled=True)
    z_below, z_above, lo_below, lo_above, lo_far, there, here, far_term = together(
        (z_below, z_above, lo_below, lo_above, lo_far, there, here, far_term)
    )
    combined = square(
        (rows, z_above, z_far, z_below, lo, lo_above, lo_far, lo_below),
        (here, there, move(here, CORE), move(there, CORE)),
    )

    z_far, lo = move(combined, Z_FAR), move(combined, Y_LO)
    z_above, z_below = move(combined, Z_DOWN), move(combined, Z_UP)
    far_term = move(far_term, Y_HI)
    z_far, lo, z_above, z_below, far_term = together((z_far, lo, z_above, z_below, far_term))
    lo_below, lo_above, lo_far = move(lo, Z_UP), move(lo, Z_DOWN), move(z_far, Y_LO)
    momentum_next = momentum_of(momentum, terms, far_term)
    lo_below, lo_above, lo_far, momentum_next = together(
        (lo_below, lo_above, lo_far, momentum_next)
    )
    mine, theirs = update_of(
        (combined, z_above, z_far, z_below, lo, lo_above, lo_far, lo_below),
        (own, above, far, below, across, across_above, across_far, across_below),
        (own_other, above_other, far_other, below_other, across_other)
        + (above_swapped, far_swapped, below_swapped),
    )
    update = lax.dynamic_update_slice(mine, move(theirs, CORE), ((1 - core) * HALF, 0))
    return (momentum_next, update)


def solution(mesh):
    parts = jax.sharding.Mesh(mesh.devices.reshape(2, 4, 16), ("y_hi", "x", "grid"))
    dp = ("y_hi", "x")
    rows, both = P(dp, None), P(dp, "grid")
    return jax.shard_map(
        per_device,
        mesh=parts,
        in_specs=(rows, both, rows, rows, both, both, both, both),
        out_specs=(both, both),
        check_vma=False,
    )
```
